512 devices in a mesh: row: 32 (over z_hi, y), col: 16 (over z_lo, x, core).
Axes of the slice: x: 4, y: 8, z: 8 (z_hi: 4, z_lo: 2; z = z_hi * 2 + z_lo), core: 2. Of those that a mesh axis runs over, the one named last changes fastest.
Arguments:
- a_blocks: bfloat16 [512, 16, 2, 128, 128], P('row', 'col'), may hold values from -6 to 6
- a_cols: int32 [512, 16, 2], P('row', 'col'), may hold values from 0 to 31, as said below
- b_blocks: bfloat16 [32, 512, 2, 128, 128], P('row', 'col'), as said below
- b_rows: int32 [32, 512, 2], P('row', 'col'), may hold values from 0 to 31, as said below
- out_cols: int32 [512, 16, 3], P('row', 'col'), may hold values from 0 to 31, as said below
Outputs:
- product: bfloat16 [512, 16, 3, 128, 128], P('row', 'col')
The draws below stay inside these ranges and needn't reach their ends.
Inputs may be any that keep to these rules, and one draw needn't show every extreme that they name: `a_cols`: the 2 indices of one block row in one slot are distinct. The 2 indices of one block column are distinct, and b_rows[q] equals b_rows[q + 16]. b_blocks[q] equals b_blocks[q + 16]. `out_cols`: the 3 kept columns of one block row in one column group are distinct.
All inputs are finite; a program needn't handle non-finite values.
Results may differ from the reference program's by a relative error of at most 0.001.
Values may be sent and summed in bfloat16 or wider, within the bound.
No kernel may reach another device: no remote copies, remote signals or barrier semaphores. Data moves between devices by JAX's collectives and lax.ppermute only.
A program may use at most 64 MiB of HBM per device.

```python
import jax
import jax.numpy as jnp
from jax import lax

BS = 128
NB = 512
KA = 2
KB = 2
KC = 3
STEPS = 4
ROW_GROUPS = 32
COL_GROUPS = 16
BC = 32
N_ROW = 32
N_COL = 16


def shared_labels(key):
    row_labels = jax.random.permutation(jax.random.fold_in(key, 101), BC).astype(jnp.int32)
    col_labels = jax.random.permutation(jax.random.fold_in(key, 103), BC).astype(jnp.int32)
    return (row_labels, col_labels)


def draw_a_cols(key, part):
    row_labels, col_labels = shared_labels(key)
    key = jax.random.fold_in(key, 11)
    spacing = jax.random.randint(key, (NB, COL_GROUPS, KA), 1, 5)
    offsets = jnp.cumsum(spacing, axis=2) - 1
    anchor = (jnp.arange(NB, dtype=jnp.int32) % BC)[:, None, None]
    position = ((anchor + offsets) % BC).astype(jnp.int32)
    return row_labels[position].astype(jnp.int32)


def draw_b_rows(key, part):
    row_labels, col_labels = shared_labels(key)
    key = jax.random.fold_in(key, 23)
    spacing = jax.random.randint(key, (COL_GROUPS, NB, KB), 1, 4)
    offsets = jnp.cumsum(spacing, axis=2) - 1
    col_inverse = jnp.argsort(col_labels).astype(jnp.int32)
    anchor = col_inverse[jnp.arange(NB, dtype=jnp.int32) % BC][None, :, None]
    position = ((anchor + offsets) % BC).astype(jnp.int32)
    single = row_labels[position].astype(jnp.int32)
    return jnp.tile(single, (ROW_GROUPS // COL_GROUPS, 1, 1))


def draw_b_blocks(key, part):
    block_key = jax.random.fold_in(key, 37)
    single = jax.random.normal(block_key, (COL_GROUPS, NB, KB, BS, BS), jnp.float32)
    single = single * BS ** (-0.5)
    return jnp.tile(single, (ROW_GROUPS // COL_GROUPS, 1, 1, 1, 1)).astype(jnp.bfloat16)


def draw_out_cols(key, part):
    row_labels, col_labels = shared_labels(key)
    key = jax.random.fold_in(key, 53)
    spacing = jax.random.randint(key, (NB, COL_GROUPS, KC), 1, 3)
    offsets = jnp.cumsum(spacing, axis=2) - 1
    anchor = (jnp.arange(NB, dtype=jnp.int32) % BC)[:, None, None]
    position = ((anchor + offsets) % BC).astype(jnp.int32)
    return col_labels[position].astype(jnp.int32)


def steps_of(rng, shape, split, least, top_value):
    def one(axis_at, blocks):
        heights = jax.random.uniform(jax.random.fold_in(jax.random.fold_in(rng, 6), axis_at), (blocks,), jnp.float32, least / len(split), top_value / len(split))
        return jnp.repeat(jnp.exp(heights), shape[axis_at] // blocks).reshape((-1,) + (1,) * (len(shape) - axis_at - 1))

    level = one(*split[0])
    for cut in split[1:]:
        level = level * one(*cut)
    return level


def noise(stream_key, shape, width, bound, cuts=(), held_as=jnp.bfloat16):
    entries = width * jax.random.normal(stream_key, shape, jnp.float32)
    if cuts:
        entries = entries * steps_of(stream_key, shape, cuts, -0.22, 0.18)
    return jnp.clip(entries, -bound, bound).astype(held_as)


def setup_inputs(seed: int = 0) -> dict:
    key_list = jax.random.split(jax.random.key(seed), 6)
    a_blocks = noise(key_list[0], (NB, COL_GROUPS, KA, BS, BS), 1.0, 6.0, ((0, 32), (1, 16)))
    a_cols = draw_a_cols(jax.random.fold_in(key_list[5], 71), 0)
    b_blocks = draw_b_blocks(jax.random.fold_in(key_list[5], 71), 0)
    b_rows = draw_b_rows(jax.random.fold_in(key_list[5], 71), 0)
    out_cols = draw_out_cols(jax.random.fold_in(key_list[5], 71), 0)
    return dict(a_blocks=a_blocks, a_cols=a_cols, b_blocks=b_blocks, b_rows=b_rows, out_cols=out_cols)


def reference(a_blocks, a_cols, b_blocks, b_rows, out_cols):
    rows_group = NB // N_ROW
    cols_group = NB // N_COL

    def one_group(group):
        start = group * rows_group
        a_group = lax.dynamic_slice_in_dim(a_blocks, start, rows_group, 0)
        ka_group = lax.dynamic_slice_in_dim(a_cols, start, rows_group, 0)
        kept = lax.dynamic_slice_in_dim(out_cols, start, rows_group, 0)
        column_ids = jnp.arange(N_COL, dtype=jnp.int32)[None, :, None] * cols_group + kept
        total = jnp.zeros((rows_group, N_COL, KC, BS, BS), jnp.float32)
        for step in range(STEPS):
            a_here = jnp.roll(a_group, -step, axis=1).astype(jnp.float32)
            ka_here = jnp.roll(ka_group, -step, axis=1)
            holder = ((group + step) % N_ROW).astype(jnp.int32)
            b_here = lax.dynamic_index_in_dim(b_blocks, holder, 0, keepdims=False)
            kb_here = lax.dynamic_index_in_dim(b_rows, holder, 0, keepdims=False)
            picked = b_here[column_ids].astype(jnp.float32)
            picked_k = kb_here[column_ids]
            match = ka_here[:, :, :, None, None] == picked_k[:, :, None, :, :]
            weights = jnp.sum(jnp.where(match[..., None, None], picked[:, :, None], jnp.float32(0.0)), axis=4)
            total = total + jnp.einsum('rcaxy,rcaoyz->rcoxz', a_here, weights)
        return total

    groups = jnp.arange(N_ROW, dtype=jnp.int32)
    result = lax.map(one_group, groups)
    return result.reshape((NB, N_COL, KC, BS, BS)).astype(jnp.bfloat16)
```

```python
import functools

import jax
import jax.numpy as jnp
from jax import lax
from jax.experimental import pallas as pl
from jax.experimental.pallas import tpu as pltpu
from jax.sharding import PartitionSpec as P

STEPS = 4
HALF = 16
RING = 8
AXES = ("row", "col")


def positions(mesh_rows, mesh_cols, place):
    pairs = []
    for row in range(mesh_rows):
        for col in range(mesh_cols):
            from_row, from_col = place(row, col)
            pairs.append(((from_row % mesh_rows) * mesh_cols + from_col % mesh_cols, row * mesh_cols + col))
    return pairs


def ahead(row, col, n_col):
    other = (row + 1) % RING == 0 and col >= n_col // 2
    return row + 1 + (HALF if other else 0)


def block_kernel(first, last, sizes, *refs):
    cols, ka, kb, a = refs[:4]
    parts = refs[4 : 4 + len(sizes)]
    rest = refs[4 + len(sizes) :]
    total = None if first else rest[0]
    out, held, sems = rest[-3:]
    copies = []
    at = 0
    for n, (part, size) in enumerate(zip(parts, sizes)):
        copies.append(pltpu.make_async_copy(part, held.at[pl.ds(at, size)], sems.at[n]))
        at += size
    for copy in copies:
        copy.start()
    held[at] = jnp.zeros(held.shape[1:], held.dtype)
    for copy in copies:
        copy.wait()
    kept = cols.shape[1]

    @pl.loop(0, a.shape[0], unroll=4)
    def _(i):
        left = jnp.concatenate([a[i, 0], a[i, 1]], axis=1)
        right = []
        for o in range(kept):
            j = cols[i, o]
            low, high = kb[j, 0], kb[j, 1]
            column = []
            for k in range(2):
                want = ka[i, k]
                place = jnp.where(low == want, 2 * j, jnp.where(high == want, 2 * j + 1, at))
                column.append(held[place])
            right.append(jnp.concatenate(column, axis=0))
        made = jnp.dot(left, jnp.concatenate(right, axis=1), preferred_element_type=jnp.float32)
        for o in range(kept):
            value = made[:, o * 128 : (o + 1) * 128]
            if not first:
                value = value + total[i, o]
            out[i, o] = value.astype(out.dtype)


def contribute(total, cols, ka, kb, a, parts, last):
    rows, kept = cols.shape
    size = a.shape[2]
    sizes = tuple(p.shape[0] for p in parts)
    first = total is None
    smem = pl.BlockSpec(memory_space=pltpu.SMEM)
    vmem = pl.BlockSpec(memory_space=pltpu.VMEM)
    whole = pl.BlockSpec(memory_space=pl.ANY)
    blocks = sum(sizes)
    return pl.pallas_call(
        functools.partial(block_kernel, first, last, sizes),
        out_shape=jax.ShapeDtypeStruct((rows, kept, size, size), jnp.bfloat16 if last else jnp.float32),
        in_specs=[smem] * 3 + [vmem] + [whole] * len(parts) + ([] if first else [vmem]),
        out_specs=vmem,
        scratch_shapes=[
            pltpu.VMEM((blocks + 1, size, size), jnp.bfloat16),
            pltpu.SemaphoreType.DMA((len(parts),)),
        ],
        compiler_params=pltpu.CompilerParams(vmem_limit_bytes=24 * 2**20),
        cost_estimate=pl.CostEstimate(
            flops=rows * kept * 4 * size**3, bytes_accessed=10 * 2**20, transcendentals=0
        ),
    )(cols, ka, kb, a, *parts, *(() if first else (total,)))


def local(n_row, n_col, a_blocks, a_cols, b_blocks, b_rows, out_cols):
    cols = out_cols[:, 0]
    ka = [a_cols[:, 0]]
    kb = [b_rows[0]]
    a_now = a_blocks[:, 0]
    blocks = b_blocks.shape[1] * b_blocks.shape[2]
    b_now = b_blocks[0].reshape((blocks,) + b_blocks.shape[3:])
    down = positions(n_row, n_col, lambda row, col: (ahead(row, col, n_col), col))
    near = positions(n_row, n_col, lambda row, col: (row + 1, col))
    side = positions(n_row, n_col, lambda row, col: (row, col + 1))
    parts = [b_now]
    total = None
    for step in range(STEPS):
        total = contribute(total, cols, ka[-1], kb[-1], a_now, parts, step + 1 == STEPS)
        if step + 1 < STEPS:
            parts = [lax.ppermute(parts[0], AXES, down)]
            a_now = lax.ppermute(a_now, AXES, side)
            ka.append(lax.ppermute(ka[-1], AXES, side))
            kb.append(lax.ppermute(kb[-1], AXES, near))
    return total[:, None]


def solution(mesh):
    n_row, n_col = mesh.shape["row"], mesh.shape["col"]
    return jax.shard_map(
        functools.partial(local, n_row, n_col),
        mesh=mesh,
        in_specs=(
            P("row", "col", None, None, None),
            P("row", "col", None),
            P("row", "col", None, None, None),
            P("row", "col", None),
            P("row", "col", None),
        ),
        out_specs=P("row", "col", None, None, None),
        check_vma=False,
    )
```

```python
import functools

import jax
import jax.numpy as jnp
from jax import lax
from jax.experimental import pallas as pl
from jax.experimental.pallas import tpu as pltpu
from jax.sharding import PartitionSpec as P

STEPS = 4
HALF = 16
RING = 8
AXES = ("row", "col")
CUT = 44


def block_kernel(first, sizes, *refs):
    cols, ka, kb, a = refs[:4]
    parts = refs[4 : 4 + len(sizes)]
    rest = refs[4 + len(sizes) :]
    total = None if first else rest[0]
    out, held, sems = rest[-3:]
    copies = []
    at = 0
    for n, (part, size) in enumerate(zip(parts, sizes)):
        copies.append(pltpu.make_async_copy(part.at[pl.ds(0, size)], held.at[pl.ds(at, size)], sems.at[n]))
        at += size
    for copy in copies:
        copy.start()
    held[at] = jnp.zeros(held.shape[1:], held.dtype)
    for copy in copies:
        copy.wait()
    rows, kept = cols.shape

    @pl.loop(0, rows, unroll=4)
    def _(i):
        left = jnp.concatenate([a[2 * i], a[2 * i + 1]], axis=1)
        right = []
        for o in range(kept):
            j = cols[i, o]
            low, high = kb[2 * j], kb[2 * j + 1]
            column = []
            for k in range(2):
                want = ka[2 * i + k]
                place = jnp.where(low == want, 2 * j, jnp.where(high == want, 2 * j + 1, at))
                column.append(held[place])
            right.append(jnp.concatenate(column, axis=0))
        made = jnp.dot(left, jnp.concatenate(right, axis=1), preferred_element_type=jnp.float32)
        for o in range(kept):
            value = made[:, o * 128 : (o + 1) * 128]
            if not first:
                value = value + total[i, o]
            out[i, o] = value.astype(out.dtype)


def contribute(total, cols, ka, kb, a, parts, sizes, last):
    rows, kept = cols.shape
    size = a.shape[2]
    first = total is None
    smem = pl.BlockSpec(memory_space=pltpu.SMEM)
    vmem = pl.BlockSpec(memory_space=pltpu.VMEM)
    whole = pl.BlockSpec(memory_space=pl.ANY)
    return pl.pallas_call(
        functools.partial(block_kernel, first, sizes),
        out_shape=jax.ShapeDtypeStruct((rows, kept, size, size), jnp.bfloat16 if last else jnp.float32),
        in_specs=[smem] * 3 + [vmem] + [whole] * len(parts) + ([] if first else [vmem]),
        out_specs=vmem,
        scratch_shapes=[
            pltpu.VMEM((sum(sizes) + 1, size, size), jnp.bfloat16),
            pltpu.SemaphoreType.DMA((len(parts),)),
        ],
        compiler_params=pltpu.CompilerParams(vmem_limit_bytes=24 * 2**20),
        cost_estimate=pl.CostEstimate(
            flops=rows * kept * 4 * size**3, bytes_accessed=10 * 2**20, transcendentals=0
        ),
    )(cols, ka, kb, a, *parts, *(() if first else (total,)))


def with_indices(blocks, indices):
    flat = indices.reshape(-1).astype(blocks.dtype)
    extra = jnp.zeros((1,) + blocks.shape[1:], blocks.dtype).at[0, 0, : flat.shape[0]].set(flat)
    return jnp.concatenate([blocks, extra], axis=0)


def indices_of(blocks, count):
    return blocks[-1, 0, :count].astype(jnp.int32)


class Paths:
    def __init__(self, n_row, n_col):
        self.n_row, self.n_col = n_row, n_col
        self.down = self.pairs(lambda z, y, t: (z + t * (y == RING - 1), y + 1))
        self.up_two = self.pairs(lambda z, y, t: (z, y - 2))
        self.up_turn = self.pairs(lambda z, y, t: (z + t * (4 <= y < RING - 1), y - 2))
        self.up_in = self.pairs(lambda z, y, t: (z, y - 1))
        self.up = self.pairs(lambda z, y, t: (z - t * (y == 0), y - 1))
        self.side = [
            (row * n_col + (col + 1) % n_col, row * n_col + col) for row in range(n_row) for col in range(n_col)
        ]

    def pairs(self, source):
        made = []
        for row in range(self.n_row):
            for col in range(self.n_col):
                z, y = source(*divmod(row, RING), 1 if col < self.n_col // 2 else -1)
                from_row = z % (self.n_row // RING) * RING + y % RING
                made.append((from_row * self.n_col + col, row * self.n_col + col))
        return made


def local(paths, a_blocks, a_cols, b_blocks, b_rows, out_cols):
    cols = out_cols[:, 0]
    ka, kb = a_cols[:, 0].reshape(-1), b_rows[0].reshape(-1)
    block = b_blocks.shape[3:]
    own = b_blocks[0].reshape((-1,) + block)
    count = own.shape[0]
    send = lambda value, pairs: lax.ppermute(value, AXES, pairs)
    sizes = (CUT, count - CUT)

    most = [with_indices(own[:CUT], kb)]
    rest = own[CUT:]
    left = [with_indices(a_blocks[:, 0].reshape((-1,) + block), ka)]
    for step in range(1, STEPS):
        most.append(send(most[-1], paths.down))
        left.append(send(left[-1], paths.side))
    far = send(send(rest, paths.up_two), paths.up_turn)
    third = send(far, paths.up_in)
    second = send(third, paths.up)
    first = send(second, paths.up)
    around = [rest, first, second, third]

    total = None
    for step in range(STEPS):
        total = contribute(
            total,
            cols,
            indices_of(left[step], ka.shape[0]) if step else ka,
            indices_of(most[step], kb.shape[0]) if step else kb,
            left[step],
            [most[step], around[step]],
            sizes,
            step + 1 == STEPS,
        )
    return total[:, None]


def solution(mesh):
    paths = Paths(mesh.shape["row"], mesh.shape["col"])
    return jax.shard_map(
        functools.partial(local, paths),
        mesh=mesh,
        in_specs=(
            P("row", "col", None, None, None),
            P("row", "col", None),
            P("row", "col", None, None, None),
            P("row", "col", None),
            P("row", "col", None),
        ),
        out_specs=P("row", "col", None, None, None),
        check_vma=False,
    )
```

```python
import functools

import jax
import jax.numpy as jnp
from jax import lax
from jax.experimental import pallas as pl
from jax.experimental.pallas import tpu as pltpu
from jax.sharding import PartitionSpec as P

STEPS = 4
HALF = 16
RING = 8
AXES = ("row", "col")
CUT = 46


def block_kernel(first, flip, count, sizes, *refs):
    flip_ref, cols, ka, kb, *rest = refs
    lefts, rest = rest[:2], rest[2:]
    parts, rest = rest[: 2 * len(sizes)], rest[2 * len(sizes) :]
    total = None if first else rest[0]
    out, made_so_far, a, held, a_sems, sems = rest[-6:]
    rows, kept = cols.shape
    span = count + 1

    def left_copy(n, slot):
        return pltpu.make_async_copy(lefts[n].at[pl.ds(0, a.shape[1])], a.at[slot], a_sems.at[slot])

    copies = [[], []]
    for slot in range(2):
        at = slot * span
        for n, size in enumerate(sizes):
            part = parts[slot * len(sizes) + n]
            copies[slot].append(
                pltpu.make_async_copy(part.at[pl.ds(0, size)], held.at[pl.ds(at, size)], sems.at[slot, n])
            )
            at += size
    if flip:

        @pl.when(flip_ref[0] == 0)
        def _():
            left_copy(0, 0).start()
            left_copy(1, 1).start()

        @pl.when(flip_ref[0] != 0)
        def _():
            left_copy(1, 0).start()
            left_copy(0, 1).start()
    else:
        left_copy(0, 0).start()
        left_copy(1, 1).start()
    for copy in copies[0] + copies[1]:
        copy.start()
    for slot in range(2):
        held[slot * span + count] = jnp.zeros(held.shape[1:], held.dtype)

    for slot in range(2):
        left_copy(slot, slot).wait()
        for copy in copies[slot]:
            copy.wait()

        @pl.loop(0, rows, unroll=4)
        def _(i):
            left = jnp.concatenate([a[slot, 2 * i], a[slot, 2 * i + 1]], axis=1)
            right = []
            for o in range(kept):
                j = cols[i, o]
                low, high = kb[slot, 2 * j], kb[slot, 2 * j + 1]
                column = []
                for k in range(2):
                    want = ka[slot, 2 * i + k]
                    place = jnp.where(low == want, 2 * j, jnp.where(high == want, 2 * j + 1, count))
                    column.append(held[slot * span + place])
                right.append(jnp.concatenate(column, axis=0))
            made = jnp.dot(left, jnp.concatenate(right, axis=1), preferred_element_type=jnp.float32)
            for o in range(kept):
                value = made[:, o * 128 : (o + 1) * 128]
                if slot:
                    value = value + made_so_far[i, o]
                    out[i, o] = value.astype(out.dtype)
                else:
                    made_so_far[i, o] = value if first else value + total[i, o]


def contribute(total, flip, cols, ka, kb, lefts, parts, sizes, last):
    rows, kept = cols.shape
    block = lefts[0].shape[1:]
    count = sum(sizes)
    first = total is None
    smem = pl.BlockSpec(memory_space=pltpu.SMEM)
    vmem = pl.BlockSpec(memory_space=pltpu.VMEM)
    whole = pl.BlockSpec(memory_space=pl.ANY)
    tall = (rows, kept) + block
    flat = [part for step in parts for part in step]
    return pl.pallas_call(
        functools.partial(block_kernel, first, flip is not None, count, sizes),
        out_shape=jax.ShapeDtypeStruct(tall, jnp.bfloat16 if last else jnp.float32),
        in_specs=[smem] * 4 + [whole] * (2 + len(flat)) + ([] if first else [vmem]),
        out_specs=vmem,
        scratch_shapes=[
            pltpu.VMEM(tall, jnp.float32),
            pltpu.VMEM((2, 2 * rows) + block, jnp.bfloat16),
            pltpu.VMEM((2 * (count + 1),) + block, jnp.bfloat16),
            pltpu.SemaphoreType.DMA((2,)),
            pltpu.SemaphoreType.DMA((2, len(sizes))),
        ],
        compiler_params=pltpu.CompilerParams(vmem_limit_bytes=28 * 2**20),
        cost_estimate=pl.CostEstimate(
            flops=rows * kept * 8 * block[0] ** 3, bytes_accessed=12 * 2**20, transcendentals=0
        ),
    )(
        jnp.zeros((1,), jnp.int32) if flip is None else flip,
        cols,
        jnp.stack(ka),
        jnp.stack(kb),
        *lefts,
        *flat,
        *(() if first else (total,)),
    )


def with_indices(blocks, indices):
    flat = indices.reshape(-1).astype(blocks.dtype)
    extra = jnp.zeros((1,) + blocks.shape[1:], blocks.dtype).at[0, 0, : flat.shape[0]].set(flat)
    return jnp.concatenate([blocks, extra], axis=0)


def indices_of(blocks, count):
    return blocks[-1, 0, :count].astype(jnp.int32)


def after(value, *others):
    return lax.optimization_barrier((value, *others))


class Paths:
    def __init__(self, n_row, n_col):
        self.n_row, self.n_col = n_row, n_col
        self.down = self.pairs(lambda z, y, t: (z + t * (y == RING - 1), y + 1))
        self.up_three = self.pairs(lambda z, y, t: (z + t * (3 <= y <= 5), y - 3))
        self.up_two = self.pairs(lambda z, y, t: (z, y - 2))
        self.up = self.pairs(lambda z, y, t: (z - t * (y == 0), y - 1))
        self.side_two = self.over_columns(lambda col: col + 2)
        self.side_odd = self.over_columns(lambda col: col + (3 if col % 2 else 1))
        self.swap = self.over_columns(lambda col: col ^ 1)

    def over_columns(self, source):
        return [
            (row * self.n_col + source(col) % self.n_col, row * self.n_col + col)
            for row in range(self.n_row)
            for col in range(self.n_col)
        ]

    def pairs(self, source):
        made = []
        for row in range(self.n_row):
            for col in range(self.n_col):
                z, y = source(*divmod(row, RING), 1 if col < self.n_col // 2 else -1)
                from_row = z % (self.n_row // RING) * RING + y % RING
                made.append((from_row * self.n_col + col, row * self.n_col + col))
        return made


def local(paths, a_blocks, a_cols, b_blocks, b_rows, out_cols):
    cols = out_cols[:, 0]
    ka, kb = a_cols[:, 0].reshape(-1), b_rows[0].reshape(-1)
    block = b_blocks.shape[3:]
    own = b_blocks[0].reshape((-1,) + block)
    count = own.shape[0]
    send = lambda value, pairs: lax.ppermute(value, AXES, pairs)
    sizes = (CUT, count - CUT)

    left = with_indices(a_blocks[:, 0].reshape((-1,) + block), ka)
    left_two = send(left, paths.side_two)
    left_odd = send(left, paths.side_odd)
    left_other = send(left_two, paths.swap)
    odd = lax.axis_index("col") % 2

    rest = own[CUT:]
    most = [with_indices(own[:CUT], kb)]
    up_one = send(rest, paths.up_three)
    most.append(send(most[0], paths.down))
    ready, left_two, up_one = after(most[1], left_two, up_one)
    most[1] = ready
    most.append(send(most[1], paths.down))
    third = send(up_one, paths.up_two)
    ready, left_odd, third = after(most[2], left_odd, third)
    most[2] = ready
    most.append(send(most[2], paths.down))
    second = send(third, paths.up)
    first = send(second, paths.up)
    parts = [[most[0], rest], [most[1], first], [most[2], second], [most[3], third]]

    rows_of = lambda value: indices_of(value, kb.shape[0])
    ka_odd, ka_other = indices_of(left_odd, ka.shape[0]), indices_of(left_other, ka.shape[0])
    ka_one, ka_three = jnp.where(odd == 0, ka_odd, ka_other), jnp.where(odd == 0, ka_other, ka_odd)
    total = contribute(
        None,
        None,
        cols,
        [ka, indices_of(left_two, ka.shape[0])],
        [kb, rows_of(most[2])],
        [left, left_two],
        [parts[0], parts[2]],
        sizes,
        False,
    )
    total = contribute(
        total,
        odd.reshape(1),
        cols,
        [ka_one, ka_three],
        [rows_of(most[1]), rows_of(most[3])],
        [left_odd, left_other],
        [parts[1], parts[3]],
        sizes,
        True,
    )
    return total[:, None]


def solution(mesh):
    paths = Paths(mesh.shape["row"], mesh.shape["col"])
    return jax.shard_map(
        functools.partial(local, paths),
        mesh=mesh,
        in_specs=(
            P("row", "col", None, None, None),
            P("row", "col", None),
            P("row", "col", None, None, None),
            P("row", "col", None),
            P("row", "col", None),
        ),
        out_specs=P("row", "col", None, None, None),
        check_vma=False,
    )
```

```python
import functools

import jax
import jax.numpy as jnp
from jax import lax
from jax.experimental import pallas as pl
from jax.experimental.pallas import tpu as pltpu
from jax.sharding import PartitionSpec as P

STEPS = 4
HALF = 16
RING = 8
AXES = ("row", "col")
CUTS = (30, 44)


def block_kernel(first, flip, count, sizes, *refs):
    flip_ref, cols, ka, kb, *rest = refs
    lefts, rest = rest[:2], rest[2:]
    parts, rest = rest[: 2 * len(sizes)], rest[2 * len(sizes) :]
    total = None if first else rest[0]
    out, made_so_far, a, held, a_sems, sems = rest[-6:]
    rows, kept = cols.shape
    span = count + 1

    def left_copy(n, slot):
        return pltpu.make_async_copy(lefts[n].at[pl.ds(0, a.shape[1])], a.at[slot], a_sems.at[slot])

    copies = [[], []]
    for slot in range(2):
        at = slot * span
        for n, size in enumerate(sizes):
            part = parts[slot * len(sizes) + n]
            copies[slot].append(
                pltpu.make_async_copy(part.at[pl.ds(0, size)], held.at[pl.ds(at, size)], sems.at[slot, n])
            )
            at += size
    if flip:

        @pl.when(flip_ref[0] == 0)
        def _():
            left_copy(0, 0).start()
            left_copy(1, 1).start()

        @pl.when(flip_ref[0] != 0)
        def _():
            left_copy(1, 0).start()
            left_copy(0, 1).start()
    else:
        left_copy(0, 0).start()
        left_copy(1, 1).start()
    for copy in copies[0] + copies[1]:
        copy.start()
    for slot in range(2):
        held[slot * span + count] = jnp.zeros(held.shape[1:], held.dtype)

    for slot in range(2):
        left_copy(slot, slot).wait()
        for copy in copies[slot]:
            copy.wait()

        @pl.loop(0, rows, unroll=4)
        def _(i):
            left = jnp.concatenate([a[slot, 2 * i], a[slot, 2 * i + 1]], axis=1)
            right = []
            for o in range(kept):
                j = cols[i, o]
                low, high = kb[slot, 2 * j], kb[slot, 2 * j + 1]
                column = []
                for k in range(2):
                    want = ka[slot, 2 * i + k]
                    place = jnp.where(low == want, 2 * j, jnp.where(high == want, 2 * j + 1, count))
                    column.append(held[slot * span + place])
                right.append(jnp.concatenate(column, axis=0))
            made = jnp.dot(left, jnp.concatenate(right, axis=1), preferred_element_type=jnp.float32)
            for o in range(kept):
                value = made[:, o * 128 : (o + 1) * 128]
                if slot:
                    value = value + made_so_far[i, o]
                    out[i, o] = value.astype(out.dtype)
                else:
                    made_so_far[i, o] = value if first else value + total[i, o]


def contribute(total, flip, cols, ka, kb, lefts, parts, sizes, last):
    rows, kept = cols.shape
    block = lefts[0].shape[1:]
    count = sum(sizes)
    first = total is None
    smem = pl.BlockSpec(memory_space=pltpu.SMEM)
    vmem = pl.BlockSpec(memory_space=pltpu.VMEM)
    whole = pl.BlockSpec(memory_space=pl.ANY)
    tall = (rows, kept) + block
    flat = [part for step in parts for part in step]
    return pl.pallas_call(
        functools.partial(block_kernel, first, flip is not None, count, sizes),
        out_shape=jax.ShapeDtypeStruct(tall, jnp.bfloat16 if last else jnp.float32),
        in_specs=[smem] * 4 + [whole] * (2 + len(flat)) + ([] if first else [vmem]),
        out_specs=vmem,
        scratch_shapes=[
            pltpu.VMEM(tall, jnp.float32),
            pltpu.VMEM((2, 2 * rows) + block, jnp.bfloat16),
            pltpu.VMEM((2 * (count + 1),) + block, jnp.bfloat16),
            pltpu.SemaphoreType.DMA((2,)),
            pltpu.SemaphoreType.DMA((2, len(sizes))),
        ],
        compiler_params=pltpu.CompilerParams(vmem_limit_bytes=28 * 2**20),
        cost_estimate=pl.CostEstimate(
            flops=rows * kept * 8 * block[0] ** 3, bytes_accessed=12 * 2**20, transcendentals=0
        ),
    )(
        jnp.zeros((1,), jnp.int32) if flip is None else flip,
        cols,
        jnp.stack(ka),
        jnp.stack(kb),
        *lefts,
        *flat,
        *(() if first else (total,)),
    )


def with_indices(blocks, indices):
    flat = indices.reshape(-1).astype(blocks.dtype)
    extra = jnp.zeros((1,) + blocks.shape[1:], blocks.dtype).at[0, 0, : flat.shape[0]].set(flat)
    return jnp.concatenate([blocks, extra], axis=0)


def indices_of(blocks, count):
    return blocks[-1, 0, :count].astype(jnp.int32)


class Paths:
    def __init__(self, n_row, n_col):
        self.n_row, self.n_col = n_row, n_col
        self.down = self.pairs(lambda z, y, t: (z + t * (y == RING - 1), y + 1))
        self.ring = self.pairs(lambda z, y, t: (z, y + 1))
        self.enter = self.pairs(lambda z, y, t: (z + t, y), only=0)
        self.up_three = self.pairs(lambda z, y, t: (z + t * (3 <= y <= 5), y - 3))
        self.up_two = self.pairs(lambda z, y, t: (z, y - 2))
        self.up = self.pairs(lambda z, y, t: (z - t * (y == 0), y - 1))
        self.side_two = self.over_columns(lambda col: col + 2)
        self.side_odd = self.over_columns(lambda col: col + (3 if col % 2 else 1))
        self.swap = self.over_columns(lambda col: col ^ 1)

    def over_columns(self, source):
        return [
            (row * self.n_col + source(col) % self.n_col, row * self.n_col + col)
            for row in range(self.n_row)
            for col in range(self.n_col)
        ]

    def pairs(self, source, only=None):
        made = []
        for row in range(self.n_row):
            if only is not None and row % RING != only:
                continue
            for col in range(self.n_col):
                z, y = source(*divmod(row, RING), 1 if col < self.n_col // 2 else -1)
                from_row = z % (self.n_row // RING) * RING + y % RING
                made.append((from_row * self.n_col + col, row * self.n_col + col))
        return made


def local(paths, a_blocks, a_cols, b_blocks, b_rows, out_cols):
    cols = out_cols[:, 0]
    ka, kb = a_cols[:, 0].reshape(-1), b_rows[0].reshape(-1)
    block = b_blocks.shape[3:]
    own = b_blocks[0].reshape((-1,) + block)
    count = own.shape[0]
    send = lambda value, pairs: lax.ppermute(value, AXES, pairs)
    cut, end = CUTS
    sizes = (cut, end - cut, count - end)

    left = with_indices(a_blocks[:, 0].reshape((-1,) + block), ka)
    left_two = send(left, paths.side_two)
    left_odd = send(left, paths.side_odd)
    left_other = send(left_two, paths.swap)
    odd = lax.axis_index("col") % 2

    rest = own[end:]
    most = [with_indices(own[:cut], kb)]
    some = [own[cut:end]]
    at_edge = lax.axis_index("row") % RING == 0

    def inside(value):
        return send(jnp.where(at_edge, send(value, paths.enter), value), paths.ring)

    up_one = send(rest, paths.up_three)
    most.append(send(most[0], paths.down))
    some.append(inside(some[0]))
    most[1], some[1], left_two, left_odd, up_one = lax.optimization_barrier(
        (most[1], some[1], left_two, left_odd, up_one)
    )
    third = send(up_one, paths.up_two)
    most.append(send(most[1], paths.down))
    some.append(inside(some[1]))
    most[2], some[2], third = lax.optimization_barrier((most[2], some[2], third))
    most.append(send(most[2], paths.down))
    some.append(inside(some[2]))
    second = send(third, paths.up)
    first = send(second, paths.up)
    parts = list(zip(most, some, [rest, first, second, third]))

    rows_of = lambda value: indices_of(value, kb.shape[0])
    ka_odd, ka_other = indices_of(left_odd, ka.shape[0]), indices_of(left_other, ka.shape[0])
    ka_one, ka_three = jnp.where(odd == 0, ka_odd, ka_other), jnp.where(odd == 0, ka_other, ka_odd)
    total = contribute(
        None,
        None,
        cols,
        [ka, indices_of(left_two, ka.shape[0])],
        [kb, rows_of(most[2])],
        [left, left_two],
        [parts[0], parts[2]],
        sizes,
        False,
    )
    total = contribute(
        total,
        odd.reshape(1),
        cols,
        [ka_one, ka_three],
        [rows_of(most[1]), rows_of(most[3])],
        [left_odd, left_other],
        [parts[1], parts[3]],
        sizes,
        True,
    )
    return total[:, None]


def solution(mesh):
    paths = Paths(mesh.shape["row"], mesh.shape["col"])
    return jax.shard_map(
        functools.partial(local, paths),
        mesh=mesh,
        in_specs=(
            P("row", "col", None, None, None),
            P("row", "col", None),
            P("row", "col", None, None, None),
            P("row", "col", None),
            P("row", "col", None),
        ),
        out_specs=P("row", "col", None, None, None),
        check_vma=False,
    )
```

```python
import functools

import jax
import jax.numpy as jnp
from jax import lax
from jax.experimental import pallas as pl
from jax.experimental.pallas import tpu as pltpu
from jax.sharding import PartitionSpec as P

STEPS = 4
HALF = 16
RING = 8
AXES = ("row", "col")
CUTS = (32, 46)


def block_kernel(first, flip, count, sizes, *refs):
    flip_ref, cols, ka, kb, *rest = refs
    lefts, rest = rest[:2], rest[2:]
    parts, rest = rest[: 2 * len(sizes)], rest[2 * len(sizes) :]
    total = None if first else rest[0]
    out, made_so_far, a, held, a_sems, sems = rest[-6:]
    rows, kept = cols.shape
    span = count + 1

    def left_copy(n, slot):
        return pltpu.make_async_copy(lefts[n].at[pl.ds(0, a.shape[1])], a.at[slot], a_sems.at[slot])

    copies = [[], []]
    for slot in range(2):
        at = slot * span
        for n, size in enumerate(sizes):
            part = parts[slot * len(sizes) + n]
            copies[slot].append(
                pltpu.make_async_copy(part.at[pl.ds(0, size)], held.at[pl.ds(at, size)], sems.at[slot, n])
            )
            at += size
    if flip:

        @pl.when(flip_ref[0] == 0)
        def _():
            left_copy(0, 0).start()
            left_copy(1, 1).start()

        @pl.when(flip_ref[0] != 0)
        def _():
            left_copy(1, 0).start()
            left_copy(0, 1).start()
    else:
        left_copy(0, 0).start()
        left_copy(1, 1).start()
    for copy in copies[0] + copies[1]:
        copy.start()
    for slot in range(2):
        held[slot * span + count] = jnp.zeros(held.shape[1:], held.dtype)

    for slot in range(2):
        left_copy(slot, slot).wait()
        for copy in copies[slot]:
            copy.wait()

        @pl.loop(0, rows, unroll=4)
        def _(i):
            left = jnp.concatenate([a[slot, 2 * i], a[slot, 2 * i + 1]], axis=1)
            right = []
            for o in range(kept):
                j = cols[i, o]
                low, high = kb[slot, 2 * j], kb[slot, 2 * j + 1]
                column = []
                for k in range(2):
                    want = ka[slot, 2 * i + k]
                    place = jnp.where(low == want, 2 * j, jnp.where(high == want, 2 * j + 1, count))
                    column.append(held[slot * span + place])
                right.append(jnp.concatenate(column, axis=0))
            made = jnp.dot(left, jnp.concatenate(right, axis=1), preferred_element_type=jnp.float32)
            for o in range(kept):
                value = made[:, o * 128 : (o + 1) * 128]
                if slot:
                    value = value + made_so_far[i, o]
                    out[i, o] = value.astype(out.dtype)
                else:
                    made_so_far[i, o] = value if first else value + total[i, o]


def contribute(total, flip, cols, ka, kb, lefts, parts, sizes, last):
    rows, kept = cols.shape
    block = lefts[0].shape[1:]
    count = sum(sizes)
    first = total is None
    smem = pl.BlockSpec(memory_space=pltpu.SMEM)
    vmem = pl.BlockSpec(memory_space=pltpu.VMEM)
    whole = pl.BlockSpec(memory_space=pl.ANY)
    tall = (rows, kept) + block
    flat = [part for step in parts for part in step]
    return pl.pallas_call(
        functools.partial(block_kernel, first, flip is not None, count, sizes),
        out_shape=jax.ShapeDtypeStruct(tall, jnp.bfloat16 if last else jnp.float32),
        in_specs=[smem] * 4 + [whole] * (2 + len(flat)) + ([] if first else [vmem]),
        out_specs=vmem,
        scratch_shapes=[
            pltpu.VMEM(tall, jnp.float32),
            pltpu.VMEM((2, 2 * rows) + block, jnp.bfloat16),
            pltpu.VMEM((2 * (count + 1),) + block, jnp.bfloat16),
            pltpu.SemaphoreType.DMA((2,)),
            pltpu.SemaphoreType.DMA((2, len(sizes))),
        ],
        compiler_params=pltpu.CompilerParams(vmem_limit_bytes=28 * 2**20),
        cost_estimate=pl.CostEstimate(
            flops=rows * kept * 8 * block[0] ** 3, bytes_accessed=12 * 2**20, transcendentals=0
        ),
    )(
        jnp.zeros((1,), jnp.int32) if flip is None else flip,
        cols,
        jnp.stack(ka),
        jnp.stack(kb),
        *lefts,
        *flat,
        *(() if first else (total,)),
    )


def with_indices(blocks, indices):
    flat = indices.reshape(-1).astype(blocks.dtype)
    extra = jnp.zeros((1,) + blocks.shape[1:], blocks.dtype).at[0, 0, : flat.shape[0]].set(flat)
    return jnp.concatenate([blocks, extra], axis=0)


def indices_of(blocks, count):
    return blocks[-1, 0, :count].astype(jnp.int32)


class Paths:
    def __init__(self, n_row, n_col):
        self.n_row, self.n_col = n_row, n_col
        self.down = self.pairs(lambda z, y, t: (z + t * (y == RING - 1), y + 1))
        self.ring = self.pairs(lambda z, y, t: (z, y + 1))
        self.enter = self.pairs(lambda z, y, t: (z + t, y), only=0)
        self.up_three = self.pairs(lambda z, y, t: (z + t * (3 <= y <= 5), y - 3))
        self.up_two = self.pairs(lambda z, y, t: (z, y - 2))
        self.up = self.pairs(lambda z, y, t: (z - t * (y == 0), y - 1))
        self.side_two = self.over_columns(lambda col: col + 2)
        self.side_odd = self.over_columns(lambda col: col + (3 if col % 2 else 1))
        self.swap = self.over_columns(lambda col: col ^ 1)

    def over_columns(self, source):
        return [
            (row * self.n_col + source(col) % self.n_col, row * self.n_col + col)
            for row in range(self.n_row)
            for col in range(self.n_col)
        ]

    def pairs(self, source, only=None):
        made = []
        for row in range(self.n_row):
            if only is not None and row % RING != only:
                continue
            for col in range(self.n_col):
                z, y = source(*divmod(row, RING), 1 if col < self.n_col // 2 else -1)
                from_row = z % (self.n_row // RING) * RING + y % RING
                made.append((from_row * self.n_col + col, row * self.n_col + col))
        return made


def local(paths, a_blocks, a_cols, b_blocks, b_rows, out_cols):
    cols = out_cols[:, 0]
    ka, kb = a_cols[:, 0].reshape(-1), b_rows[0].reshape(-1)
    block = b_blocks.shape[3:]
    own = b_blocks[0].reshape((-1,) + block)
    count = own.shape[0]
    send = lambda value, pairs: lax.ppermute(value, AXES, pairs)
    cut, end = CUTS
    sizes = (cut, end - cut, count - end)

    left = with_indices(a_blocks[:, 0].reshape((-1,) + block), ka)
    left_two = send(left, paths.side_two)
    left_odd = send(left, paths.side_odd)
    left_other = send(left_two, paths.swap)
    odd = lax.axis_index("col") % 2

    rest = own[end:]
    most = [with_indices(own[:cut], kb)]
    some = [own[cut:end]]
    at_edge = lax.axis_index("row") % RING == 0

    def inside(value):
        return send(jnp.where(at_edge, send(value, paths.enter), value), paths.ring)

    up_one = send(rest, paths.up_three)
    most.append(send(most[0], paths.down))
    some.append(inside(some[0]))
    most[1], some[1], left_two, up_one = lax.optimization_barrier((most[1], some[1], left_two, up_one))
    third = send(up_one, paths.up_two)
    most.append(send(most[1], paths.down))
    some.append(inside(some[1]))
    most[2], some[2], third = lax.optimization_barrier((most[2], some[2], third))
    most.append(send(most[2], paths.down))
    some.append(inside(some[2]))
    second = send(third, paths.up)
    first = send(second, paths.up)
    most[3], some[3], first, left_odd, left_other = lax.optimization_barrier(
        (most[3], some[3], first, left_odd, left_other)
    )
    parts = list(zip(most, some, [rest, first, second, third]))

    rows_of = lambda value: indices_of(value, kb.shape[0])
    ka_odd, ka_other = indices_of(left_odd, ka.shape[0]), indices_of(left_other, ka.shape[0])
    ka_one, ka_three = jnp.where(odd == 0, ka_odd, ka_other), jnp.where(odd == 0, ka_other, ka_odd)
    total = contribute(
        None,
        None,
        cols,
        [ka, indices_of(left_two, ka.shape[0])],
        [kb, rows_of(most[2])],
        [left, left_two],
        [parts[0], parts[2]],
        sizes,
        False,
    )
    total = contribute(
        total,
        odd.reshape(1),
        cols,
        [ka_one, ka_three],
        [rows_of(most[1]), rows_of(most[3])],
        [left_odd, left_other],
        [parts[1], parts[3]],
        sizes,
        True,
    )
    return total[:, None]


def solution(mesh):
    paths = Paths(mesh.shape["row"], mesh.shape["col"])
    return jax.shard_map(
        functools.partial(local, paths),
        mesh=mesh,
        in_specs=(
            P("row", "col", None, None, None),
            P("row", "col", None),
            P("row", "col", None, None, None),
            P("row", "col", None),
            P("row", "col", None),
        ),
        out_specs=P("row", "col", None, None, None),
        check_vma=False,
    )
```

```python
import functools

import jax
import jax.numpy as jnp
from jax import lax
from jax.experimental import pallas as pl
from jax.experimental.pallas import tpu as pltpu
from jax.sharding import PartitionSpec as P

STEPS = 4
HALF = 16
RING = 8
AXES = ("row", "col")
CUTS = (32, 46)


def block_kernel(first, flip, count, sizes, *refs):
    flip_ref, cols, *rest = refs
    kas, kbs, rest = rest[:2], rest[2:4], rest[4:]
    lefts, rest = rest[:2], rest[2:]
    parts, rest = rest[: 2 * len(sizes)], rest[2 * len(sizes) :]
    total = None if first else rest[0]
    out, made_so_far, a, held, a_sems, sems = rest[-6:]
    kept, rows = cols.shape
    span = count + 1

    def left_copy(n, slot):
        return pltpu.make_async_copy(lefts[n].at[pl.ds(0, a.shape[1])], a.at[slot], a_sems.at[slot])

    copies = [[], []]
    for slot in range(2):
        at = slot * span
        for n, size in enumerate(sizes):
            part = parts[slot * len(sizes) + n]
            copies[slot].append(
                pltpu.make_async_copy(part.at[pl.ds(0, size)], held.at[pl.ds(at, size)], sems.at[slot, n])
            )
            at += size
    if flip:

        @pl.when(flip_ref[0] == 0)
        def _():
            left_copy(0, 0).start()
            left_copy(1, 1).start()

        @pl.when(flip_ref[0] != 0)
        def _():
            left_copy(1, 0).start()
            left_copy(0, 1).start()
    else:
        left_copy(0, 0).start()
        left_copy(1, 1).start()
    for copy in copies[0] + copies[1]:
        copy.start()
    for slot in range(2):
        held[slot * span + count] = jnp.zeros(held.shape[1:], held.dtype)

    for slot in range(2):
        left_copy(slot, slot).wait()
        for copy in copies[slot]:
            copy.wait()

        @pl.loop(0, rows, unroll=8)
        def _(i):
            left = jnp.concatenate([a[slot, 2 * i], a[slot, 2 * i + 1]], axis=1)
            right = []
            for o in range(kept):
                j = cols[o, i]
                low, high = kbs[slot][0, j], kbs[slot][1, j]
                column = []
                for k in range(2):
                    want = kas[slot][k, i]
                    place = jnp.where(low == want, 2 * j, jnp.where(high == want, 2 * j + 1, count))
                    column.append(held[slot * span + place])
                right.append(jnp.concatenate(column, axis=0))
            made = jnp.dot(left, jnp.concatenate(right, axis=1), preferred_element_type=jnp.float32)
            for o in range(kept):
                value = made[:, o * 128 : (o + 1) * 128]
                if slot:
                    value = value + made_so_far[i, o]
                    out[i, o] = value.astype(out.dtype)
                else:
                    made_so_far[i, o] = value if first else value + total[i, o]


def contribute(total, flip, cols, ka, kb, lefts, parts, sizes, last):
    kept, rows = cols.shape
    block = lefts[0].shape[1:]
    count = sum(sizes)
    first = total is None
    smem = pl.BlockSpec(memory_space=pltpu.SMEM)
    vmem = pl.BlockSpec(memory_space=pltpu.VMEM)
    whole = pl.BlockSpec(memory_space=pl.ANY)
    tall = (rows, kept) + block
    flat = [part for step in parts for part in step]
    return pl.pallas_call(
        functools.partial(block_kernel, first, flip is not None, count, sizes),
        out_shape=jax.ShapeDtypeStruct(tall, jnp.bfloat16 if last else jnp.float32),
        in_specs=[smem] * 6 + [whole] * (2 + len(flat)) + ([] if first else [vmem]),
        out_specs=vmem,
        scratch_shapes=[
            pltpu.VMEM(tall, jnp.float32),
            pltpu.VMEM((2, 2 * rows) + block, jnp.bfloat16),
            pltpu.VMEM((2 * (count + 1),) + block, jnp.bfloat16),
            pltpu.SemaphoreType.DMA((2,)),
            pltpu.SemaphoreType.DMA((2, len(sizes))),
        ],
        compiler_params=pltpu.CompilerParams(vmem_limit_bytes=28 * 2**20),
        cost_estimate=pl.CostEstimate(
            flops=rows * kept * 8 * block[0] ** 3, bytes_accessed=12 * 2**20, transcendentals=0
        ),
    )(
        jnp.zeros((1,), jnp.int32) if flip is None else flip,
        cols,
        *ka,
        *kb,
        *lefts,
        *flat,
        *(() if first else (total,)),
    )


def with_indices(blocks, indices):
    low, high = (blocks.shape[n] - indices.shape[n - 1] for n in (1, 2))
    extra = jnp.pad(indices.astype(blocks.dtype), ((0, low), (0, high)))
    return jnp.concatenate([blocks, extra[None]], axis=0)


def indices_of(blocks, shape):
    return blocks[-1, : shape[0], : shape[1]].astype(jnp.int32)


class Paths:
    def __init__(self, n_row, n_col):
        self.n_row, self.n_col = n_row, n_col
        self.down = self.pairs(lambda z, y, t: (z + t * (y == RING - 1), y + 1))
        self.ring = self.pairs(lambda z, y, t: (z, y + 1))
        self.enter = self.pairs(lambda z, y, t: (z + t, y), only=0)
        self.up_two = self.pairs(lambda z, y, t: (z, y - 2))
        self.up_turn = self.pairs(lambda z, y, t: (z + t * (4 <= y < RING - 1), y - 2))
        self.up_in = self.pairs(lambda z, y, t: (z, y - 1))
        self.up = self.pairs(lambda z, y, t: (z - t * (y == 0), y - 1))
        self.side_two = self.over_columns(lambda col: col + 2)
        self.side_odd = self.over_columns(lambda col: col + (3 if col % 2 else 1))
        self.swap = self.over_columns(lambda col: col ^ 1)

    def over_columns(self, source):
        return [
            (row * self.n_col + source(col) % self.n_col, row * self.n_col + col)
            for row in range(self.n_row)
            for col in range(self.n_col)
        ]

    def pairs(self, source, only=None):
        made = []
        for row in range(self.n_row):
            if only is not None and row % RING != only:
                continue
            for col in range(self.n_col):
                z, y = source(*divmod(row, RING), 1 if col < self.n_col // 2 else -1)
                from_row = z % (self.n_row // RING) * RING + y % RING
                made.append((from_row * self.n_col + col, row * self.n_col + col))
        return made


def local(paths, a_blocks, a_cols, b_blocks, b_rows, out_cols):
    cols = out_cols[:, 0].T
    ka, kb = a_cols[:, 0].T, b_rows[0].T
    block = b_blocks.shape[3:]
    own = b_blocks[0].reshape((-1,) + block)
    count = own.shape[0]
    send = lambda value, pairs: lax.ppermute(value, AXES, pairs)
    cut, end = CUTS
    sizes = (cut, end - cut, count - end)

    left = with_indices(a_blocks[:, 0].reshape((-1,) + block), ka)
    left_two = send(left, paths.side_two)
    left_odd = send(left, paths.side_odd)
    left_other = send(left_two, paths.swap)
    odd = lax.axis_index("col") % 2

    rest = own[end:]
    most = [with_indices(own[:cut], kb)]
    some = [own[cut:end]]
    at_edge = lax.axis_index("row") % RING == 0

    def inside(value):
        return send(jnp.where(at_edge, send(value, paths.enter), value), paths.ring)

    up_one = send(rest, paths.up_two)
    most.append(send(most[0], paths.down))
    some.append(inside(some[0]))
    most[1], some[1], left_two, up_one = lax.optimization_barrier((most[1], some[1], left_two, up_one))
    up_two = send(up_one, paths.up_turn)
    third = send(up_two, paths.up_in)
    most.append(send(most[1], paths.down))
    some.append(inside(some[1]))
    most[2], some[2], _ = lax.optimization_barrier((most[2], some[2], up_two))
    most.append(send(most[2], paths.down))
    some.append(inside(some[2]))
    second = send(third, paths.up)
    first = send(second, paths.up)
    parts = list(zip(most, some, [rest, first, second, third]))

    rows_of = lambda value: indices_of(value, kb.shape)
    ka_odd, ka_other = indices_of(left_odd, ka.shape), indices_of(left_other, ka.shape)
    ka_one, ka_three = jnp.where(odd == 0, ka_odd, ka_other), jnp.where(odd == 0, ka_other, ka_odd)
    total = contribute(
        None,
        None,
        cols,
        [ka, indices_of(left_two, ka.shape)],
        [kb, rows_of(most[2])],
        [left, left_two],
        [parts[0], parts[2]],
        sizes,
        False,
    )
    total = contribute(
        total,
        odd.reshape(1),
        cols,
        [ka_one, ka_three],
        [rows_of(most[1]), rows_of(most[3])],
        [left_odd, left_other],
        [parts[1], parts[3]],
        sizes,
        True,
    )
    return total[:, None]


def solution(mesh):
    paths = Paths(mesh.shape["row"], mesh.shape["col"])
    return jax.shard_map(
        functools.partial(local, paths),
        mesh=mesh,
        in_specs=(
            P("row", "col", None, None, None),
            P("row", "col", None),
            P("row", "col", None, None, None),
            P("row", "col", None),
            P("row", "col", None),
        ),
        out_specs=P("row", "col", None, None, None),
        check_vma=False,
    )
```

```python
import functools

import jax
import jax.numpy as jnp
from jax import lax
from jax.experimental import pallas as pl
from jax.experimental.pallas import tpu as pltpu
from jax.sharding import PartitionSpec as P

STEPS = 4
HALF = 16
RING = 8
AXES = ("row", "col")
CUTS = (28, 46)


def block_kernel(first, flip, count, sizes, *refs):
    flip_ref, cols, *rest = refs
    kas, kbs, rest = rest[:2], rest[2:4], rest[4:]
    lefts, rest = rest[:2], rest[2:]
    parts, rest = rest[: 2 * len(sizes)], rest[2 * len(sizes) :]
    total = None if first else rest[0]
    out, made_so_far, a, held, a_sems, sems = rest[-6:]
    kept, rows = cols.shape
    span = count + 1

    def left_copy(n, slot):
        return pltpu.make_async_copy(lefts[n].at[pl.ds(0, a.shape[1])], a.at[slot], a_sems.at[slot])

    copies = [[], []]
    for slot in range(2):
        at = slot * span
        for n, size in enumerate(sizes):
            part = parts[slot * len(sizes) + n]
            copies[slot].append(
                pltpu.make_async_copy(part.at[pl.ds(0, size)], held.at[pl.ds(at, size)], sems.at[slot, n])
            )
            at += size
    if flip:

        @pl.when(flip_ref[0] == 0)
        def _():
            left_copy(0, 0).start()
            left_copy(1, 1).start()

        @pl.when(flip_ref[0] != 0)
        def _():
            left_copy(1, 0).start()
            left_copy(0, 1).start()
    else:
        left_copy(0, 0).start()
        left_copy(1, 1).start()
    for copy in copies[0] + copies[1]:
        copy.start()
    for slot in range(2):
        held[slot * span + count] = jnp.zeros(held.shape[1:], held.dtype)

    for slot in range(2):
        left_copy(slot, slot).wait()
        for copy in copies[slot]:
            copy.wait()

        @pl.loop(0, rows, unroll=8)
        def _(i):
            left = jnp.concatenate([a[slot, 2 * i], a[slot, 2 * i + 1]], axis=1)
            right = []
            for o in range(kept):
                j = cols[o, i]
                low, high = kbs[slot][0, j], kbs[slot][1, j]
                column = []
                for k in range(2):
                    want = kas[slot][k, i]
                    place = jnp.where(low == want, 2 * j, jnp.where(high == want, 2 * j + 1, count))
                    column.append(held[slot * span + place])
                right.append(jnp.concatenate(column, axis=0))
            made = jnp.dot(left, jnp.concatenate(right, axis=1), preferred_element_type=jnp.float32)
            for o in range(kept):
                value = made[:, o * 128 : (o + 1) * 128]
                if slot:
                    value = value + made_so_far[i, o]
                    out[i, o] = value.astype(out.dtype)
                else:
                    made_so_far[i, o] = value if first else value + total[i, o]


def contribute(total, flip, cols, ka, kb, lefts, parts, sizes, last):
    kept, rows = cols.shape
    block = lefts[0].shape[1:]
    count = sum(sizes)
    first = total is None
    smem = pl.BlockSpec(memory_space=pltpu.SMEM)
    vmem = pl.BlockSpec(memory_space=pltpu.VMEM)
    whole = pl.BlockSpec(memory_space=pl.ANY)
    tall = (rows, kept) + block
    flat = [part for step in parts for part in step]
    return pl.pallas_call(
        functools.partial(block_kernel, first, flip is not None, count, sizes),
        out_shape=jax.ShapeDtypeStruct(tall, jnp.bfloat16 if last else jnp.float32),
        in_specs=[smem] * 6 + [whole] * (2 + len(flat)) + ([] if first else [vmem]),
        out_specs=vmem,
        scratch_shapes=[
            pltpu.VMEM(tall, jnp.float32),
            pltpu.VMEM((2, 2 * rows) + block, jnp.bfloat16),
            pltpu.VMEM((2 * (count + 1),) + block, jnp.bfloat16),
            pltpu.SemaphoreType.DMA((2,)),
            pltpu.SemaphoreType.DMA((2, len(sizes))),
        ],
        compiler_params=pltpu.CompilerParams(vmem_limit_bytes=28 * 2**20),
        cost_estimate=pl.CostEstimate(
            flops=rows * kept * 8 * block[0] ** 3, bytes_accessed=12 * 2**20, transcendentals=0
        ),
    )(
        jnp.zeros((1,), jnp.int32) if flip is None else flip,
        cols,
        *ka,
        *kb,
        *lefts,
        *flat,
        *(() if first else (total,)),
    )


def with_indices(blocks, indices):
    low, high = (blocks.shape[n] - indices.shape[n - 1] for n in (1, 2))
    extra = jnp.pad(indices.astype(blocks.dtype), ((0, low), (0, high)))
    return jnp.concatenate([blocks, extra[None]], axis=0)


def indices_of(blocks, shape):
    return blocks[-1, : shape[0], : shape[1]].astype(jnp.int32)


class Paths:
    def __init__(self, n_row, n_col):
        self.n_row, self.n_col = n_row, n_col
        self.down = self.pairs(lambda z, y, t: (z + t * (y == RING - 1), y + 1))
        self.ring = self.pairs(lambda z, y, t: (z, y + 1))
        self.enter = self.pairs(lambda z, y, t: (z + t, y), only=0)
        self.up_two = self.pairs(lambda z, y, t: (z, y - 2))
        self.up_turn = self.pairs(lambda z, y, t: (z + t * (4 <= y < RING - 1), y - 2))
        self.up_in = self.pairs(lambda z, y, t: (z, y - 1))
        self.up = self.pairs(lambda z, y, t: (z - t * (y == 0), y - 1))
        self.side_two = self.over_columns(lambda col: col + 2)
        self.side_odd = self.over_columns(lambda col: col + (3 if col % 2 else 1))
        self.swap = self.over_columns(lambda col: col ^ 1)

    def over_columns(self, source):
        return [
            (row * self.n_col + source(col) % self.n_col, row * self.n_col + col)
            for row in range(self.n_row)
            for col in range(self.n_col)
        ]

    def pairs(self, source, only=None):
        made = []
        for row in range(self.n_row):
            if only is not None and row % RING != only:
                continue
            for col in range(self.n_col):
                z, y = source(*divmod(row, RING), 1 if col < self.n_col // 2 else -1)
                from_row = z % (self.n_row // RING) * RING + y % RING
                made.append((from_row * self.n_col + col, row * self.n_col + col))
        return made


def local(paths, a_blocks, a_cols, b_blocks, b_rows, out_cols):
    cols = out_cols[:, 0].T
    ka, kb = a_cols[:, 0].T, b_rows[0].T
    block = b_blocks.shape[3:]
    own = b_blocks[0].reshape((-1,) + block)
    count = own.shape[0]
    send = lambda value, pairs: lax.ppermute(value, AXES, pairs)
    cut, end = CUTS
    sizes = (cut, end - cut, count - end)

    left = with_indices(a_blocks[:, 0].reshape((-1,) + block), ka)
    left_two = send(left, paths.side_two)
    left_odd = send(left, paths.side_odd)
    left_other = send(left_two, paths.swap)
    odd = lax.axis_index("col") % 2

    rest = own[end:]
    most = [with_indices(own[:cut], kb)]
    some = [own[cut:end]]
    at_edge = lax.axis_index("row") % RING == 0

    def inside(value):
        return send(jnp.where(at_edge, send(value, paths.enter), value), paths.ring)

    up_one = send(rest, paths.up_two)
    most.append(send(most[0], paths.down))
    some.append(inside(some[0]))
    most[1], some[1], left_two, up_one = lax.optimization_barrier((most[1], some[1], left_two, up_one))
    up_two = send(up_one, paths.up_turn)
    third = send(up_two, paths.up_in)
    most.append(send(most[1], paths.down))
    some.append(inside(some[1]))
    most[2], some[2], _ = lax.optimization_barrier((most[2], some[2], up_two))
    most.append(send(most[2], paths.down))
    some.append(inside(some[2]))
    second = send(third, paths.up)
    first = send(second, paths.up)
    parts = list(zip(most, some, [rest, first, second, third]))

    rows_of = lambda value: indices_of(value, kb.shape)
    ka_odd, ka_other = indices_of(left_odd, ka.shape), indices_of(left_other, ka.shape)
    ka_one, ka_three = jnp.where(odd == 0, ka_odd, ka_other), jnp.where(odd == 0, ka_other, ka_odd)
    total = contribute(
        None,
        None,
        cols,
        [ka, indices_of(left_two, ka.shape)],
        [kb, rows_of(most[2])],
        [left, left_two],
        [parts[0], parts[2]],
        sizes,
        False,
    )
    total = contribute(
        total,
        odd.reshape(1),
        cols,
        [ka_one, ka_three],
        [rows_of(most[1]), rows_of(most[3])],
        [left_odd, left_other],
        [parts[1], parts[3]],
        sizes,
        True,
    )
    return total[:, None]


def solution(mesh):
    paths = Paths(mesh.shape["row"], mesh.shape["col"])
    return jax.shard_map(
        functools.partial(local, paths),
        mesh=mesh,
        in_specs=(
            P("row", "col", None, None, None),
            P("row", "col", None),
            P("row", "col", None, None, None),
            P("row", "col", None),
            P("row", "col", None),
        ),
        out_specs=P("row", "col", None, None, None),
        check_vma=False,
    )
```

```python
import functools

import jax
import jax.numpy as jnp
from jax import lax
from jax.experimental import pallas as pl
from jax.experimental.pallas import tpu as pltpu
from jax.sharding import PartitionSpec as P

STEPS = 4
HALF = 16
RING = 8
AXES = ("row", "col")
CUTS = (30, 46)


def block_kernel(first, flip, count, sizes, *refs):
    flip_ref, cols, *rest = refs
    kas, kbs, rest = rest[:2], rest[2:4], rest[4:]
    lefts, rest = rest[:2], rest[2:]
    parts, rest = rest[: 2 * len(sizes)], rest[2 * len(sizes) :]
    total = None if first else rest[0]
    out, made_so_far, a, held, a_sems, sems = rest[-6:]
    kept, rows = cols.shape
    span = count + 1

    def left_copy(n, slot):
        return pltpu.make_async_copy(lefts[n].at[pl.ds(0, a.shape[1])], a.at[slot], a_sems.at[slot])

    copies = [[], []]
    for slot in range(2):
        at = slot * span
        for n, size in enumerate(sizes):
            part = parts[slot * len(sizes) + n]
            copies[slot].append(
                pltpu.make_async_copy(part.at[pl.ds(0, size)], held.at[pl.ds(at, size)], sems.at[slot, n])
            )
            at += size
    if flip:

        @pl.when(flip_ref[0] == 0)
        def _():
            left_copy(0, 0).start()
            left_copy(1, 1).start()

        @pl.when(flip_ref[0] != 0)
        def _():
            left_copy(1, 0).start()
            left_copy(0, 1).start()
    else:
        left_copy(0, 0).start()
        left_copy(1, 1).start()
    for copy in copies[0] + copies[1]:
        copy.start()
    for slot in range(2):
        held[slot * span + count] = jnp.zeros(held.shape[1:], held.dtype)

    for slot in range(2):
        left_copy(slot, slot).wait()
        for copy in copies[slot]:
            copy.wait()

        @pl.loop(0, rows, unroll=16)
        def _(i):
            left = jnp.concatenate([a[slot, 2 * i], a[slot, 2 * i + 1]], axis=1)
            right = []
            for o in range(kept):
                j = cols[o, i]
                low, high = kbs[slot][0, j], kbs[slot][1, j]
                column = []
                for k in range(2):
                    want = kas[slot][k, i]
                    place = jnp.where(low == want, 2 * j, jnp.where(high == want, 2 * j + 1, count))
                    column.append(held[slot * span + place])
                right.append(jnp.concatenate(column, axis=0))
            made = jnp.dot(left, jnp.concatenate(right, axis=1), preferred_element_type=jnp.float32)
            for o in range(kept):
                value = made[:, o * 128 : (o + 1) * 128]
                if slot:
                    value = value + made_so_far[i, o]
                    out[i, o] = value.astype(out.dtype)
                else:
                    made_so_far[i, o] = value if first else value + total[i, o]


def contribute(total, flip, cols, ka, kb, lefts, parts, sizes, last):
    kept, rows = cols.shape
    block = lefts[0].shape[1:]
    count = sum(sizes)
    first = total is None
    smem = pl.BlockSpec(memory_space=pltpu.SMEM)
    vmem = pl.BlockSpec(memory_space=pltpu.VMEM)
    whole = pl.BlockSpec(memory_space=pl.ANY)
    tall = (rows, kept) + block
    flat = [part for step in parts for part in step]
    return pl.pallas_call(
        functools.partial(block_kernel, first, flip is not None, count, sizes),
        out_shape=jax.ShapeDtypeStruct(tall, jnp.bfloat16 if last else jnp.float32),
        in_specs=[smem] * 6 + [whole] * (2 + len(flat)) + ([] if first else [vmem]),
        out_specs=vmem,
        scratch_shapes=[
            pltpu.VMEM(tall, jnp.float32),
            pltpu.VMEM((2, 2 * rows) + block, jnp.bfloat16),
            pltpu.VMEM((2 * (count + 1),) + block, jnp.bfloat16),
            pltpu.SemaphoreType.DMA((2,)),
            pltpu.SemaphoreType.DMA((2, len(sizes))),
        ],
        compiler_params=pltpu.CompilerParams(vmem_limit_bytes=28 * 2**20),
        cost_estimate=pl.CostEstimate(
            flops=rows * kept * 8 * block[0] ** 3, bytes_accessed=12 * 2**20, transcendentals=0
        ),
    )(
        jnp.zeros((1,), jnp.int32) if flip is None else flip,
        cols,
        *ka,
        *kb,
        *lefts,
        *flat,
        *(() if first else (total,)),
    )


def with_indices(blocks, indices):
    low, high = (blocks.shape[n] - indices.shape[n - 1] for n in (1, 2))
    extra = jnp.pad(indices.astype(blocks.dtype), ((0, low), (0, high)))
    return jnp.concatenate([blocks, extra[None]], axis=0)


def indices_of(blocks, shape):
    return blocks[-1, : shape[0], : shape[1]].astype(jnp.int32)


class Paths:
    def __init__(self, n_row, n_col):
        self.n_row, self.n_col = n_row, n_col
        self.down = self.pairs(lambda z, y, t: (z + t * (y == RING - 1), y + 1))
        self.ring = self.pairs(lambda z, y, t: (z, y + 1))
        self.enter = self.pairs(lambda z, y, t: (z + t, y), only=0)
        self.up_two = self.pairs(lambda z, y, t: (z, y - 2))
        self.up_turn = self.pairs(lambda z, y, t: (z + t * (4 <= y < RING - 1), y - 2))
        self.up_in = self.pairs(lambda z, y, t: (z, y - 1))
        self.up = self.pairs(lambda z, y, t: (z - t * (y == 0), y - 1))
        self.side_two = self.over_columns(lambda col: col + 2)
        self.side_odd = self.over_columns(lambda col: col + (3 if col % 2 else 1))
        self.swap = self.over_columns(lambda col: col ^ 1)

    def over_columns(self, source):
        return [
            (row * self.n_col + source(col) % self.n_col, row * self.n_col + col)
            for row in range(self.n_row)
            for col in range(self.n_col)
        ]

    def pairs(self, source, only=None):
        made = []
        for row in range(self.n_row):
            if only is not None and row % RING != only:
                continue
            for col in range(self.n_col):
                z, y = source(*divmod(row, RING), 1 if col < self.n_col // 2 else -1)
                from_row = z % (self.n_row // RING) * RING + y % RING
                made.append((from_row * self.n_col + col, row * self.n_col + col))
        return made


def local(paths, a_blocks, a_cols, b_blocks, b_rows, out_cols):
    cols = out_cols[:, 0].T
    ka, kb = a_cols[:, 0].T, b_rows[0].T
    block = b_blocks.shape[3:]
    own = b_blocks[0].reshape((-1,) + block)
    count = own.shape[0]
    send = lambda value, pairs: lax.ppermute(value, AXES, pairs)
    cut, end = CUTS
    sizes = (cut, end - cut, count - end)

    left = with_indices(a_blocks[:, 0].reshape((-1,) + block), ka)
    left_two = send(left, paths.side_two)
    left_odd = send(left, paths.side_odd)
    left_other = send(left_two, paths.swap)
    odd = lax.axis_index("col") % 2

    rest = own[end:]
    most = [with_indices(own[:cut], kb)]
    some = [own[cut:end]]
    at_edge = lax.axis_index("row") % RING == 0

    def inside(value):
        return send(jnp.where(at_edge, send(value, paths.enter), value), paths.ring)

    up_one = send(rest, paths.up_two)
    most.append(send(most[0], paths.down))
    some.append(inside(some[0]))
    most[1], some[1], left_two, up_one = lax.optimization_barrier((most[1], some[1], left_two, up_one))
    up_two = send(up_one, paths.up_turn)
    third = send(up_two, paths.up_in)
    most.append(send(most[1], paths.down))
    some.append(inside(some[1]))
    most[2], some[2], left_odd, _ = lax.optimization_barrier((most[2], some[2], left_odd, up_two))
    most.append(send(most[2], paths.down))
    some.append(inside(some[2]))
    second = send(third, paths.up)
    first = send(second, paths.up)
    parts = list(zip(most, some, [rest, first, second, third]))

    rows_of = lambda value: indices_of(value, kb.shape)
    ka_odd, ka_other = indices_of(left_odd, ka.shape), indices_of(left_other, ka.shape)
    ka_one, ka_three = jnp.where(odd == 0, ka_odd, ka_other), jnp.where(odd == 0, ka_other, ka_odd)
    total = contribute(
        None,
        None,
        cols,
        [ka, indices_of(left_two, ka.shape)],
        [kb, rows_of(most[2])],
        [left, left_two],
        [parts[0], parts[2]],
        sizes,
        False,
    )
    total = contribute(
        total,
        odd.reshape(1),
        cols,
        [ka_one, ka_three],
        [rows_of(most[1]), rows_of(most[3])],
        [left_odd, left_other],
        [parts[1], parts[3]],
        sizes,
        True,
    )
    return total[:, None]


def solution(mesh):
    paths = Paths(mesh.shape["row"], mesh.shape["col"])
    return jax.shard_map(
        functools.partial(local, paths),
        mesh=mesh,
        in_specs=(
            P("row", "col", None, None, None),
            P("row", "col", None),
            P("row", "col", None, None, None),
            P("row", "col", None),
            P("row", "col", None),
        ),
        out_specs=P("row", "col", None, None, None),
        check_vma=False,
    )
```

```python
import functools

import jax
import jax.numpy as jnp
from jax import lax
from jax.experimental import pallas as pl
from jax.experimental.pallas import tpu as pltpu
from jax.sharding import PartitionSpec as P

STEPS = 4
HALF = 16
RING = 8
AXES = ("row", "col")
CUTS = (28, 46)


def block_kernel(first, flip, count, sizes, *refs):
    flip_ref, cols, *rest = refs
    kas, kbs, rest = rest[:2], rest[2:4], rest[4:]
    lefts, rest = rest[:2], rest[2:]
    parts, rest = rest[: 2 * len(sizes)], rest[2 * len(sizes) :]
    total = None if first else rest[0]
    out, made_so_far, a, held, a_sems, sems = rest[-6:]
    kept, rows = cols.shape
    span = count + 1

    def left_copy(n, slot):
        return pltpu.make_async_copy(lefts[n].at[pl.ds(0, a.shape[1])], a.at[slot], a_sems.at[slot])

    copies = [[], []]
    for slot in range(2):
        at = slot * span
        for n, size in enumerate(sizes):
            part = parts[slot * len(sizes) + n]
            copies[slot].append(
                pltpu.make_async_copy(part.at[pl.ds(0, size)], held.at[pl.ds(at, size)], sems.at[slot, n])
            )
            at += size
    if flip:

        @pl.when(flip_ref[0] == 0)
        def _():
            left_copy(0, 0).start()
            left_copy(1, 1).start()

        @pl.when(flip_ref[0] != 0)
        def _():
            left_copy(1, 0).start()
            left_copy(0, 1).start()
    else:
        left_copy(0, 0).start()
        left_copy(1, 1).start()
    for copy in copies[0] + copies[1]:
        copy.start()
    for slot in range(2):
        held[slot * span + count] = jnp.zeros(held.shape[1:], held.dtype)

    for slot in range(2):
        left_copy(slot, slot).wait()
        for copy in copies[slot]:
            copy.wait()

        @pl.loop(0, rows, unroll=16)
        def _(i):
            left = jnp.concatenate([a[slot, 2 * i], a[slot, 2 * i + 1]], axis=1)
            right = []
            for o in range(kept):
                j = cols[o, i]
                low, high = kbs[slot][0, j], kbs[slot][1, j]
                column = []
                for k in range(2):
                    want = kas[slot][k, i]
                    place = jnp.where(low == want, 2 * j, jnp.where(high == want, 2 * j + 1, count))
                    column.append(held[slot * span + place])
                right.append(jnp.concatenate(column, axis=0))
            made = jnp.dot(left, jnp.concatenate(right, axis=1), preferred_element_type=jnp.float32)
            for o in range(kept):
                value = made[:, o * 128 : (o + 1) * 128]
                if slot:
                    value = value + made_so_far[i, o]
                    out[i, o] = value.astype(out.dtype)
                else:
                    made_so_far[i, o] = value if first else value + total[i, o]


def contribute(total, flip, cols, ka, kb, lefts, parts, sizes, last):
    kept, rows = cols.shape
    block = lefts[0].shape[1:]
    count = sum(sizes)
    first = total is None
    smem = pl.BlockSpec(memory_space=pltpu.SMEM)
    vmem = pl.BlockSpec(memory_space=pltpu.VMEM)
    whole = pl.BlockSpec(memory_space=pl.ANY)
    tall = (rows, kept) + block
    flat = [part for step in parts for part in step]
    return pl.pallas_call(
        functools.partial(block_kernel, first, flip is not None, count, sizes),
        out_shape=jax.ShapeDtypeStruct(tall, jnp.bfloat16 if last else jnp.float32),
        in_specs=[smem] * 6 + [whole] * (2 + len(flat)) + ([] if first else [vmem]),
        out_specs=vmem,
        scratch_shapes=[
            pltpu.VMEM(tall, jnp.float32),
            pltpu.VMEM((2, 2 * rows) + block, jnp.bfloat16),
            pltpu.VMEM((2 * (count + 1),) + block, jnp.bfloat16),
            pltpu.SemaphoreType.DMA((2,)),
            pltpu.SemaphoreType.DMA((2, len(sizes))),
        ],
        compiler_params=pltpu.CompilerParams(vmem_limit_bytes=28 * 2**20),
        cost_estimate=pl.CostEstimate(
            flops=rows * kept * 8 * block[0] ** 3, bytes_accessed=12 * 2**20, transcendentals=0
        ),
    )(
        jnp.zeros((1,), jnp.int32) if flip is None else flip,
        cols,
        *ka,
        *kb,
        *lefts,
        *flat,
        *(() if first else (total,)),
    )


def with_indices(blocks, indices):
    low, high = (blocks.shape[n] - indices.shape[n - 1] for n in (1, 2))
    extra = jnp.pad(indices.astype(blocks.dtype), ((0, low), (0, high)))
    return jnp.concatenate([blocks, extra[None]], axis=0)


def indices_of(blocks, shape):
    return blocks[-1, : shape[0], : shape[1]].astype(jnp.int32)


class Paths:
    def __init__(self, n_row, n_col):
        self.n_row, self.n_col = n_row, n_col
        self.down = self.pairs(lambda z, y, t: (z + t * (y == RING - 1), y + 1))
        self.ring = self.pairs(lambda z, y, t: (z, y + 1))
        self.enter = self.pairs(lambda z, y, t: (z + t, y), only=0)
        self.up_two = self.pairs(lambda z, y, t: (z, y - 2))
        self.up_turn = self.pairs(lambda z, y, t: (z + t * (4 <= y < RING - 1), y - 2))
        self.up_in = self.pairs(lambda z, y, t: (z, y - 1))
        self.up = self.pairs(lambda z, y, t: (z - t * (y == 0), y - 1))
        self.side_two = self.over_columns(lambda col: col + 2)
        self.side_odd = self.over_columns(lambda col: col + (3 if col % 2 else 1))
        self.swap = self.over_columns(lambda col: col ^ 1)

    def over_columns(self, source):
        return [
            (row * self.n_col + source(col) % self.n_col, row * self.n_col + col)
            for row in range(self.n_row)
            for col in range(self.n_col)
        ]

    def pairs(self, source, only=None):
        made = []
        for row in range(self.n_row):
            if only is not None and row % RING != only:
                continue
            for col in range(self.n_col):
                z, y = source(*divmod(row, RING), 1 if col < self.n_col // 2 else -1)
                from_row = z % (self.n_row // RING) * RING + y % RING
                made.append((from_row * self.n_col + col, row * self.n_col + col))
        return made


def local(paths, a_blocks, a_cols, b_blocks, b_rows, out_cols):
    cols = out_cols[:, 0].T
    ka, kb = a_cols[:, 0].T, b_rows[0].T
    block = b_blocks.shape[3:]
    own = b_blocks[0].reshape((-1,) + block)
    count = own.shape[0]
    send = lambda value, pairs: lax.ppermute(value, AXES, pairs)
    cut, end = CUTS
    sizes = (cut, end - cut, count - end)

    left = with_indices(a_blocks[:, 0].reshape((-1,) + block), ka)
    left_two = send(left, paths.side_two)
    left_odd = send(left, paths.side_odd)
    left_other = send(left_two, paths.swap)
    odd = lax.axis_index("col") % 2

    rest = own[end:]
    most = [with_indices(own[:cut], kb)]
    some = [own[cut:end]]
    at_edge = lax.axis_index("row") % RING == 0

    def inside(value):
        return send(jnp.where(at_edge, send(value, paths.enter), value), paths.ring)

    up_one = send(rest, paths.up_two)
    most.append(send(most[0], paths.down))
    some.append(inside(some[0]))
    most[1], some[1], left_two, up_one = lax.optimization_barrier((most[1], some[1], left_two, up_one))
    up_two = send(up_one, paths.up_turn)
    third = send(up_two, paths.up_in)
    most.append(send(most[1], paths.down))
    some.append(inside(some[1]))
    most[2], some[2], _ = lax.optimization_barrier((most[2], some[2], up_two))
    most.append(send(most[2], paths.down))
    some.append(send(some[2], paths.down))
    later, _ = lax.optimization_barrier((third, most[2]))
    second = send(later, paths.up)
    first = send(second, paths.up)
    parts = list(zip(most, some, [rest, first, second, third]))

    rows_of = lambda value: indices_of(value, kb.shape)
    ka_odd, ka_other = indices_of(left_odd, ka.shape), indices_of(left_other, ka.shape)
    ka_one, ka_three = jnp.where(odd == 0, ka_odd, ka_other), jnp.where(odd == 0, ka_other, ka_odd)
    total = contribute(
        None,
        None,
        cols,
        [ka, indices_of(left_two, ka.shape)],
        [kb, rows_of(most[2])],
        [left, left_two],
        [parts[0], parts[2]],
        sizes,
        False,
    )
    total = contribute(
        total,
        odd.reshape(1),
        cols,
        [ka_one, ka_three],
        [rows_of(most[1]), rows_of(most[3])],
        [left_odd, left_other],
        [parts[1], parts[3]],
        sizes,
        True,
    )
    return total[:, None]


def solution(mesh):
    paths = Paths(mesh.shape["row"], mesh.shape["col"])
    return jax.shard_map(
        functools.partial(local, paths),
        mesh=mesh,
        in_specs=(
            P("row", "col", None, None, None),
            P("row", "col", None),
            P("row", "col", None, None, None),
            P("row", "col", None),
            P("row", "col", None),
        ),
        out_specs=P("row", "col", None, None, None),
        check_vma=False,
    )
```

```python
import functools

import jax
import jax.numpy as jnp
from jax import lax
from jax.experimental import pallas as pl
from jax.experimental.pallas import tpu as pltpu
from jax.sharding import PartitionSpec as P

STEPS = 4
HALF = 16
RING = 8
AXES = ("row", "col")
CUTS = (28, 46)


def block_kernel(first, flip, count, sizes, begins, *refs):
    flip_ref, cols, *rest = refs
    kas, kbs, rest = rest[:2], rest[2:4], rest[4:]
    lefts, rest = rest[:2], rest[2:]
    parts, rest = rest[: 2 * len(sizes)], rest[2 * len(sizes) :]
    total = None if first else rest[0]
    out, made_so_far, a, held, a_sems, sems = rest[-6:]
    kept, rows = cols.shape
    span = count + 1

    def left_copy(n, slot):
        return pltpu.make_async_copy(lefts[n].at[pl.ds(0, a.shape[1])], a.at[slot], a_sems.at[slot])

    copies = [[], []]
    for slot in range(2):
        at = slot * span
        for n, size in enumerate(sizes):
            part = parts[slot * len(sizes) + n]
            copies[slot].append(
                pltpu.make_async_copy(part.at[pl.ds(begins[slot][n], size)], held.at[pl.ds(at, size)], sems.at[slot, n])
            )
            at += size
    if flip:

        @pl.when(flip_ref[0] == 0)
        def _():
            left_copy(0, 0).start()
            left_copy(1, 1).start()

        @pl.when(flip_ref[0] != 0)
        def _():
            left_copy(1, 0).start()
            left_copy(0, 1).start()
    else:
        left_copy(0, 0).start()
        left_copy(1, 1).start()
    for copy in copies[0] + copies[1]:
        copy.start()
    for slot in range(2):
        held[slot * span + count] = jnp.zeros(held.shape[1:], held.dtype)

    for slot in range(2):
        left_copy(slot, slot).wait()
        for copy in copies[slot]:
            copy.wait()

        @pl.loop(0, rows, unroll=16)
        def _(i):
            left = jnp.concatenate([a[slot, 2 * i], a[slot, 2 * i + 1]], axis=1)
            right = []
            for o in range(kept):
                j = cols[o, i]
                low, high = kbs[slot][0, j], kbs[slot][1, j]
                column = []
                for k in range(2):
                    want = kas[slot][k, i]
                    place = jnp.where(low == want, 2 * j, jnp.where(high == want, 2 * j + 1, count))
                    column.append(held[slot * span + place])
                right.append(jnp.concatenate(column, axis=0))
            made = jnp.dot(left, jnp.concatenate(right, axis=1), preferred_element_type=jnp.float32)
            for o in range(kept):
                value = made[:, o * 128 : (o + 1) * 128]
                if slot:
                    value = value + made_so_far[i, o]
                    out[i, o] = value.astype(out.dtype)
                else:
                    made_so_far[i, o] = value if first else value + total[i, o]


def contribute(total, flip, cols, ka, kb, lefts, parts, sizes, begins, last):
    kept, rows = cols.shape
    block = lefts[0].shape[1:]
    count = sum(sizes)
    first = total is None
    smem = pl.BlockSpec(memory_space=pltpu.SMEM)
    vmem = pl.BlockSpec(memory_space=pltpu.VMEM)
    whole = pl.BlockSpec(memory_space=pl.ANY)
    tall = (rows, kept) + block
    flat = [part for step in parts for part in step]
    return pl.pallas_call(
        functools.partial(block_kernel, first, flip is not None, count, sizes, begins),
        out_shape=jax.ShapeDtypeStruct(tall, jnp.bfloat16 if last else jnp.float32),
        in_specs=[smem] * 6 + [whole] * (2 + len(flat)) + ([] if first else [vmem]),
        out_specs=vmem,
        scratch_shapes=[
            pltpu.VMEM(tall, jnp.float32),
            pltpu.VMEM((2, 2 * rows) + block, jnp.bfloat16),
            pltpu.VMEM((2 * (count + 1),) + block, jnp.bfloat16),
            pltpu.SemaphoreType.DMA((2,)),
            pltpu.SemaphoreType.DMA((2, len(sizes))),
        ],
        compiler_params=pltpu.CompilerParams(vmem_limit_bytes=28 * 2**20),
        cost_estimate=pl.CostEstimate(
            flops=rows * kept * 8 * block[0] ** 3, bytes_accessed=12 * 2**20, transcendentals=0
        ),
    )(
        jnp.zeros((1,), jnp.int32) if flip is None else flip,
        cols,
        *ka,
        *kb,
        *lefts,
        *flat,
        *(() if first else (total,)),
    )


def with_indices(blocks, indices):
    low, high = (blocks.shape[n] - indices.shape[n - 1] for n in (1, 2))
    extra = jnp.pad(indices.astype(blocks.dtype), ((0, low), (0, high)))
    return jnp.concatenate([blocks, extra[None]], axis=0)


def indices_of(blocks, shape, at=-1):
    return blocks[at, : shape[0], : shape[1]].astype(jnp.int32)


class Paths:
    def __init__(self, n_row, n_col):
        self.n_row, self.n_col = n_row, n_col
        self.down = self.pairs(lambda z, y, t: (z + t * (y == RING - 1), y + 1))
        self.ring = self.pairs(lambda z, y, t: (z, y + 1))
        self.enter = self.pairs(lambda z, y, t: (z + t, y), only=0)
        self.up_two = self.pairs(lambda z, y, t: (z, y - 2))
        self.up_turn = self.pairs(lambda z, y, t: (z + t * (4 <= y < RING - 1), y - 2))
        self.up_in = self.pairs(lambda z, y, t: (z, y - 1))
        self.up = self.pairs(lambda z, y, t: (z - t * (y == 0), y - 1))
        self.side_two = self.over_columns(lambda col: col + 2)
        self.side_odd = self.over_columns(lambda col: col + (3 if col % 2 else 1))
        self.swap = self.over_columns(lambda col: col ^ 1)

    def over_columns(self, source):
        return [
            (row * self.n_col + source(col) % self.n_col, row * self.n_col + col)
            for row in range(self.n_row)
            for col in range(self.n_col)
        ]

    def pairs(self, source, only=None):
        made = []
        for row in range(self.n_row):
            if only is not None and row % RING != only:
                continue
            for col in range(self.n_col):
                z, y = source(*divmod(row, RING), 1 if col < self.n_col // 2 else -1)
                from_row = z % (self.n_row // RING) * RING + y % RING
                made.append((from_row * self.n_col + col, row * self.n_col + col))
        return made


def local(paths, a_blocks, a_cols, b_blocks, b_rows, out_cols):
    cols = out_cols[:, 0].T
    ka, kb = a_cols[:, 0].T, b_rows[0].T
    block = b_blocks.shape[3:]
    own = b_blocks[0].reshape((-1,) + block)
    count = own.shape[0]
    send = lambda value, pairs: lax.ppermute(value, AXES, pairs)
    cut, end = CUTS
    sizes = (cut, end - cut, count - end)

    left = with_indices(a_blocks[:, 0].reshape((-1,) + block), ka)
    left_two = send(left, paths.side_two)
    left_odd = send(left, paths.side_odd)
    left_other = send(left_two, paths.swap)
    odd = lax.axis_index("col") % 2

    rest = own[end:]
    most = [with_indices(own[:cut], kb)]
    some = [own[cut:end]]
    at_edge = lax.axis_index("row") % RING == 0

    def inside(value):
        return send(jnp.where(at_edge, send(value, paths.enter), value), paths.ring)

    up_one = send(rest, paths.up_two)
    most.append(send(most[0], paths.down))
    some.append(inside(some[0]))
    most[1], some[1], left_two, up_one = lax.optimization_barrier((most[1], some[1], left_two, up_one))
    up_two = send(up_one, paths.up_turn)
    third = send(up_two, paths.up_in)
    most.append(send(most[1], paths.down))
    some.append(inside(some[1]))
    most[2], some[2], _ = lax.optimization_barrier((most[2], some[2], up_two))
    both = send(jnp.concatenate([most[2], some[2]], axis=0), paths.down)
    most.append(both)
    some.append(both)
    later, _ = lax.optimization_barrier((third, most[2]))
    second = send(later, paths.up)
    first = send(second, paths.up)
    parts = list(zip(most, some, [rest, first, second, third]))

    rows_of = lambda value: indices_of(value, kb.shape)
    ka_odd, ka_other = indices_of(left_odd, ka.shape), indices_of(left_other, ka.shape)
    ka_one, ka_three = jnp.where(odd == 0, ka_odd, ka_other), jnp.where(odd == 0, ka_other, ka_odd)
    total = contribute(
        None,
        None,
        cols,
        [ka, indices_of(left_two, ka.shape)],
        [kb, rows_of(most[2])],
        [left, left_two],
        [parts[0], parts[2]],
        sizes,
        ((0, 0, 0), (0, 0, 0)),
        False,
    )
    total = contribute(
        total,
        odd.reshape(1),
        cols,
        [ka_one, ka_three],
        [rows_of(most[1]), indices_of(both, kb.shape, cut)],
        [left_odd, left_other],
        [parts[1], parts[3]],
        sizes,
        ((0, 0, 0), (0, cut + 1, 0)),
        True,
    )
    return total[:, None]


def solution(mesh):
    paths = Paths(mesh.shape["row"], mesh.shape["col"])
    return jax.shard_map(
        functools.partial(local, paths),
        mesh=mesh,
        in_specs=(
            P("row", "col", None, None, None),
            P("row", "col", None),
            P("row", "col", None, None, None),
            P("row", "col", None),
            P("row", "col", None),
        ),
        out_specs=P("row", "col", None, None, None),
        check_vma=False,
    )
```

```python
import functools

import jax
import jax.numpy as jnp
from jax import lax
from jax.experimental import pallas as pl
from jax.experimental.pallas import tpu as pltpu
from jax.sharding import PartitionSpec as P

STEPS = 4
HALF = 16
RING = 8
AXES = ("row", "col")
CUTS = (30, 47)


def block_kernel(first, flip, count, sizes, begins, *refs):
    flip_ref, cols, *rest = refs
    kas, kbs, rest = rest[:2], rest[2:4], rest[4:]
    lefts, rest = rest[:2], rest[2:]
    parts, rest = rest[: 2 * len(sizes)], rest[2 * len(sizes) :]
    total = None if first else rest[0]
    out, made_so_far, a, held, a_sems, sems = rest[-6:]
    kept, rows = cols.shape
    span = count + 1

    def left_copy(n, slot):
        return pltpu.make_async_copy(lefts[n].at[pl.ds(0, a.shape[1])], a.at[slot], a_sems.at[slot])

    copies = [[], []]
    for slot in range(2):
        at = slot * span
        for n, size in enumerate(sizes):
            part = parts[slot * len(sizes) + n]
            copies[slot].append(
                pltpu.make_async_copy(part.at[pl.ds(begins[slot][n], size)], held.at[pl.ds(at, size)], sems.at[slot, n])
            )
            at += size
    if flip:

        @pl.when(flip_ref[0] == 0)
        def _():
            left_copy(0, 0).start()
            left_copy(1, 1).start()

        @pl.when(flip_ref[0] != 0)
        def _():
            left_copy(1, 0).start()
            left_copy(0, 1).start()
    else:
        left_copy(0, 0).start()
        left_copy(1, 1).start()
    for copy in copies[0] + copies[1]:
        copy.start()
    for slot in range(2):
        held[slot * span + count] = jnp.zeros(held.shape[1:], held.dtype)

    for slot in range(2):
        left_copy(slot, slot).wait()
        for copy in copies[slot]:
            copy.wait()

        @pl.loop(0, rows, unroll=16)
        def _(i):
            left = jnp.concatenate([a[slot, 2 * i], a[slot, 2 * i + 1]], axis=1)
            right = []
            for o in range(kept):
                j = cols[o, i]
                low, high = kbs[slot][0, j], kbs[slot][1, j]
                column = []
                for k in range(2):
                    want = kas[slot][k, i]
                    place = jnp.where(low == want, 2 * j, jnp.where(high == want, 2 * j + 1, count))
                    column.append(held[slot * span + place])
                right.append(jnp.concatenate(column, axis=0))
            made = jnp.dot(left, jnp.concatenate(right, axis=1), preferred_element_type=jnp.float32)
            for o in range(kept):
                value = made[:, o * 128 : (o + 1) * 128]
                if slot:
                    value = value + made_so_far[i, o]
                    out[i, o] = value.astype(out.dtype)
                else:
                    made_so_far[i, o] = value if first else value + total[i, o]


def contribute(total, flip, cols, ka, kb, lefts, parts, sizes, begins, last):
    kept, rows = cols.shape
    block = lefts[0].shape[1:]
    count = sum(sizes)
    first = total is None
    smem = pl.BlockSpec(memory_space=pltpu.SMEM)
    vmem = pl.BlockSpec(memory_space=pltpu.VMEM)
    whole = pl.BlockSpec(memory_space=pl.ANY)
    tall = (rows, kept) + block
    flat = [part for step in parts for part in step]
    return pl.pallas_call(
        functools.partial(block_kernel, first, flip is not None, count, sizes, begins),
        out_shape=jax.ShapeDtypeStruct(tall, jnp.bfloat16 if last else jnp.float32),
        in_specs=[smem] * 6 + [whole] * (2 + len(flat)) + ([] if first else [vmem]),
        out_specs=vmem,
        scratch_shapes=[
            pltpu.VMEM(tall, jnp.float32),
            pltpu.VMEM((2, 2 * rows) + block, jnp.bfloat16),
            pltpu.VMEM((2 * (count + 1),) + block, jnp.bfloat16),
            pltpu.SemaphoreType.DMA((2,)),
            pltpu.SemaphoreType.DMA((2, len(sizes))),
        ],
        compiler_params=pltpu.CompilerParams(vmem_limit_bytes=28 * 2**20),
        cost_estimate=pl.CostEstimate(
            flops=rows * kept * 8 * block[0] ** 3, bytes_accessed=12 * 2**20, transcendentals=0
        ),
    )(
        jnp.zeros((1,), jnp.int32) if flip is None else flip,
        cols,
        *ka,
        *kb,
        *lefts,
        *flat,
        *(() if first else (total,)),
    )


def with_indices(blocks, indices):
    low, high = (blocks.shape[n] - indices.shape[n - 1] for n in (1, 2))
    extra = jnp.pad(indices.astype(blocks.dtype), ((0, low), (0, high)))
    return jnp.concatenate([blocks, extra[None]], axis=0)


def indices_of(blocks, shape, at=-1):
    return blocks[at, : shape[0], : shape[1]].astype(jnp.int32)


class Paths:
    def __init__(self, n_row, n_col):
        self.n_row, self.n_col = n_row, n_col
        self.down = self.pairs(lambda z, y, t: (z + t * (y == RING - 1), y + 1))
        self.ring = self.pairs(lambda z, y, t: (z, y + 1))
        self.enter = self.pairs(lambda z, y, t: (z + t, y), only=0)
        self.up_two = self.pairs(lambda z, y, t: (z, y - 2))
        self.up_turn = self.pairs(lambda z, y, t: (z + t * (4 <= y < RING - 1), y - 2))
        self.up_in = self.pairs(lambda z, y, t: (z, y - 1))
        self.up = self.pairs(lambda z, y, t: (z - t * (y == 0), y - 1))
        self.side_two = self.over_columns(lambda col: col + 2)
        self.side_odd = self.over_columns(lambda col: col + (3 if col % 2 else 1))
        self.swap = self.over_columns(lambda col: col ^ 1)

    def over_columns(self, source):
        return [
            (row * self.n_col + source(col) % self.n_col, row * self.n_col + col)
            for row in range(self.n_row)
            for col in range(self.n_col)
        ]

    def pairs(self, source, only=None):
        made = []
        for row in range(self.n_row):
            if only is not None and row % RING != only:
                continue
            for col in range(self.n_col):
                z, y = source(*divmod(row, RING), 1 if col < self.n_col // 2 else -1)
                from_row = z % (self.n_row // RING) * RING + y % RING
                made.append((from_row * self.n_col + col, row * self.n_col + col))
        return made


def local(paths, a_blocks, a_cols, b_blocks, b_rows, out_cols):
    cols = out_cols[:, 0].T
    ka, kb = a_cols[:, 0].T, b_rows[0].T
    block = b_blocks.shape[3:]
    own = b_blocks[0].reshape((-1,) + block)
    count = own.shape[0]
    send = lambda value, pairs: lax.ppermute(value, AXES, pairs)
    cut, end = CUTS
    sizes = (cut, end - cut, count - end)

    left = with_indices(a_blocks[:, 0].reshape((-1,) + block), ka)
    left_two = send(left, paths.side_two)
    left_odd = send(left, paths.side_odd)
    left_other = send(left_two, paths.swap)
    odd = lax.axis_index("col") % 2

    rest = own[end:]
    most = [with_indices(own[:cut], kb)]
    some = [own[cut:end]]
    at_edge = lax.axis_index("row") % RING == 0

    def inside(value):
        return send(jnp.where(at_edge, send(value, paths.enter), value), paths.ring)

    up_one = send(rest, paths.up_two)
    most.append(send(most[0], paths.down))
    some.append(inside(some[0]))
    most[1], some[1], left_two, up_one = lax.optimization_barrier((most[1], some[1], left_two, up_one))
    up_two = send(up_one, paths.up_turn)
    third = send(up_two, paths.up_in)
    most.append(send(most[1], paths.down))
    some.append(inside(some[1]))
    most[2], some[2], _ = lax.optimization_barrier((most[2], some[2], up_two))
    both = send(jnp.concatenate([most[2], some[2]], axis=0), paths.down)
    most.append(both)
    some.append(both)
    later, _ = lax.optimization_barrier((third, most[2]))
    second = send(later, paths.up)
    first = send(second, paths.up)
    parts = list(zip(most, some, [rest, first, second, third]))

    rows_of = lambda value: indices_of(value, kb.shape)
    ka_odd, ka_other = indices_of(left_odd, ka.shape), indices_of(left_other, ka.shape)
    ka_one, ka_three = jnp.where(odd == 0, ka_odd, ka_other), jnp.where(odd == 0, ka_other, ka_odd)
    total = contribute(
        None,
        None,
        cols,
        [ka, indices_of(left_two, ka.shape)],
        [kb, rows_of(most[2])],
        [left, left_two],
        [parts[0], parts[2]],
        sizes,
        ((0, 0, 0), (0, 0, 0)),
        False,
    )
    total = contribute(
        total,
        odd.reshape(1),
        cols,
        [ka_one, ka_three],
        [rows_of(most[1]), indices_of(both, kb.shape, cut)],
        [left_odd, left_other],
        [parts[1], parts[3]],
        sizes,
        ((0, 0, 0), (0, cut + 1, 0)),
        True,
    )
    return total[:, None]


def solution(mesh):
    paths = Paths(mesh.shape["row"], mesh.shape["col"])
    return jax.shard_map(
        functools.partial(local, paths),
        mesh=mesh,
        in_specs=(
            P("row", "col", None, None, None),
            P("row", "col", None),
            P("row", "col", None, None, None),
            P("row", "col", None),
            P("row", "col", None),
        ),
        out_specs=P("row", "col", None, None, None),
        check_vma=False,
    )
```

```python
import functools

import jax
import jax.numpy as jnp
from jax import lax
from jax.experimental import pallas as pl
from jax.experimental.pallas import tpu as pltpu
from jax.sharding import PartitionSpec as P

STEPS = 4
HALF = 16
RING = 8
AXES = ("row", "col")
CUTS = (30, 48)


def block_kernel(first, flip, count, sizes, *refs):
    flip_ref, cols, *rest = refs
    kas, kbs, rest = rest[:2], rest[2:4], rest[4:]
    lefts, rest = rest[:2], rest[2:]
    parts, rest = rest[: 2 * len(sizes)], rest[2 * len(sizes) :]
    total = None if first else rest[0]
    out, made_so_far, a, held, a_sems, sems = rest[-6:]
    kept, rows = cols.shape
    span = count + 1

    def left_copy(n, slot):
        return pltpu.make_async_copy(lefts[n].at[pl.ds(0, a.shape[1])], a.at[slot], a_sems.at[slot])

    copies = [[], []]
    for slot in range(2):
        at = slot * span
        for n, size in enumerate(sizes):
            part = parts[slot * len(sizes) + n]
            copies[slot].append(
                pltpu.make_async_copy(part.at[pl.ds(0, size)], held.at[pl.ds(at, size)], sems.at[slot, n])
            )
            at += size
    if flip:

        @pl.when(flip_ref[0] == 0)
        def _():
            left_copy(0, 0).start()
            left_copy(1, 1).start()

        @pl.when(flip_ref[0] != 0)
        def _():
            left_copy(1, 0).start()
            left_copy(0, 1).start()
    else:
        left_copy(0, 0).start()
        left_copy(1, 1).start()
    for copy in copies[0] + copies[1]:
        copy.start()
    for slot in range(2):
        held[slot * span + count] = jnp.zeros(held.shape[1:], held.dtype)

    for slot in range(2):
        left_copy(slot, slot).wait()
        for copy in copies[slot]:
            copy.wait()

        @pl.loop(0, rows, unroll=16)
        def _(i):
            left = jnp.concatenate([a[slot, 2 * i], a[slot, 2 * i + 1]], axis=1)
            right = []
            for o in range(kept):
                j = cols[o, i]
                low, high = kbs[slot][0, j], kbs[slot][1, j]
                column = []
                for k in range(2):
                    want = kas[slot][k, i]
                    place = jnp.where(low == want, 2 * j, jnp.where(high == want, 2 * j + 1, count))
                    column.append(held[slot * span + place])
                right.append(jnp.concatenate(column, axis=0))
            made = jnp.dot(left, jnp.concatenate(right, axis=1), preferred_element_type=jnp.float32)
            for o in range(kept):
                value = made[:, o * 128 : (o + 1) * 128]
                if slot:
                    value = value + made_so_far[i, o]
                    out[i, o] = value.astype(out.dtype)
                else:
                    made_so_far[i, o] = value if first else value + total[i, o]


def contribute(total, flip, cols, ka, kb, lefts, parts, sizes, last):
    kept, rows = cols.shape
    block = lefts[0].shape[1:]
    count = sum(sizes)
    first = total is None
    smem = pl.BlockSpec(memory_space=pltpu.SMEM)
    vmem = pl.BlockSpec(memory_space=pltpu.VMEM)
    whole = pl.BlockSpec(memory_space=pl.ANY)
    tall = (rows, kept) + block
    flat = [part for step in parts for part in step]
    return pl.pallas_call(
        functools.partial(block_kernel, first, flip is not None, count, sizes),
        out_shape=jax.ShapeDtypeStruct(tall, jnp.bfloat16 if last else jnp.float32),
        in_specs=[smem] * 6 + [whole] * (2 + len(flat)) + ([] if first else [vmem]),
        out_specs=vmem,
        scratch_shapes=[
            pltpu.VMEM(tall, jnp.float32),
            pltpu.VMEM((2, 2 * rows) + block, jnp.bfloat16),
            pltpu.VMEM((2 * (count + 1),) + block, jnp.bfloat16),
            pltpu.SemaphoreType.DMA((2,)),
            pltpu.SemaphoreType.DMA((2, len(sizes))),
        ],
        compiler_params=pltpu.CompilerParams(vmem_limit_bytes=28 * 2**20),
        cost_estimate=pl.CostEstimate(
            flops=rows * kept * 8 * block[0] ** 3, bytes_accessed=12 * 2**20, transcendentals=0
        ),
    )(
        jnp.zeros((1,), jnp.int32) if flip is None else flip,
        cols,
        *ka,
        *kb,
        *lefts,
        *flat,
        *(() if first else (total,)),
    )


def with_indices(blocks, indices):
    low, high = (blocks.shape[n] - indices.shape[n - 1] for n in (1, 2))
    extra = jnp.pad(indices.astype(blocks.dtype), ((0, low), (0, high)))
    return jnp.concatenate([blocks, extra[None]], axis=0)


def indices_of(blocks, shape):
    return blocks[-1, : shape[0], : shape[1]].astype(jnp.int32)


class Paths:
    def __init__(self, n_row, n_col):
        self.n_row, self.n_col = n_row, n_col
        self.down = self.pairs(lambda z, y, t: (z + t * (y == RING - 1), y + 1))
        self.ring = self.pairs(lambda z, y, t: (z, y + 1))
        self.enter = self.pairs(lambda z, y, t: (z + t, y), only=0)
        self.up_two = self.pairs(lambda z, y, t: (z, y - 2))
        self.up_turn = self.pairs(lambda z, y, t: (z + t * (4 <= y < RING - 1), y - 2))
        self.up_in = self.pairs(lambda z, y, t: (z, y - 1))
        self.up = self.pairs(lambda z, y, t: (z - t * (y == 0), y - 1))
        self.side_two = self.over_columns(lambda col: col + 2)
        self.side_odd = self.over_columns(lambda col: col + (3 if col % 2 else 1))
        self.swap = self.over_columns(lambda col: col ^ 1)

    def over_columns(self, source):
        return [
            (row * self.n_col + source(col) % self.n_col, row * self.n_col + col)
            for row in range(self.n_row)
            for col in range(self.n_col)
        ]

    def pairs(self, source, only=None):
        made = []
        for row in range(self.n_row):
            if only is not None and row % RING != only:
                continue
            for col in range(self.n_col):
                z, y = source(*divmod(row, RING), 1 if col < self.n_col // 2 else -1)
                from_row = z % (self.n_row // RING) * RING + y % RING
                made.append((from_row * self.n_col + col, row * self.n_col + col))
        return made


def local(paths, a_blocks, a_cols, b_blocks, b_rows, out_cols):
    cols = out_cols[:, 0].T
    ka, kb = a_cols[:, 0].T, b_rows[0].T
    block = b_blocks.shape[3:]
    own = b_blocks[0].reshape((-1,) + block)
    count = own.shape[0]
    send = lambda value, pairs: lax.ppermute(value, AXES, pairs)
    cut, end = CUTS
    sizes = (cut, end - cut, count - end)

    left = with_indices(a_blocks[:, 0].reshape((-1,) + block), ka)
    left_two = send(left, paths.side_two)
    left_odd = send(left, paths.side_odd)
    left_other = send(left_two, paths.swap)
    odd = lax.axis_index("col") % 2

    rest = own[end:]
    most = [with_indices(own[:cut], kb)]
    some = [own[cut:end]]
    at_edge = lax.axis_index("row") % RING == 0

    def inside(value):
        return send(jnp.where(at_edge, send(value, paths.enter), value), paths.ring)

    up_one = send(rest, paths.up_two)
    most.append(send(most[0], paths.down))
    some.append(inside(some[0]))
    most[1], some[1], left_two, up_one = lax.optimization_barrier((most[1], some[1], left_two, up_one))
    up_two = send(up_one, paths.up_turn)
    third = send(up_two, paths.up_in)
    most.append(send(most[1], paths.down))
    some.append(inside(some[1]))
    most[2], some[2], _ = lax.optimization_barrier((most[2], some[2], up_two))
    most.append(send(most[2], paths.down))
    some.append(send(some[2], paths.down))
    later, _ = lax.optimization_barrier((third, most[2]))
    second = send(later, paths.up)
    first = send(second, paths.up)
    parts = list(zip(most, some, [rest, first, second, third]))

    rows_of = lambda value: indices_of(value, kb.shape)
    ka_odd, ka_other = indices_of(left_odd, ka.shape), indices_of(left_other, ka.shape)
    ka_one, ka_three = jnp.where(odd == 0, ka_odd, ka_other), jnp.where(odd == 0, ka_other, ka_odd)
    total = contribute(
        None,
        None,
        cols,
        [ka, indices_of(left_two, ka.shape)],
        [kb, rows_of(most[2])],
        [left, left_two],
        [parts[0], parts[2]],
        sizes,
        False,
    )
    total = contribute(
        total,
        odd.reshape(1),
        cols,
        [ka_one, ka_three],
        [rows_of(most[1]), rows_of(most[3])],
        [left_odd, left_other],
        [parts[1], parts[3]],
        sizes,
        True,
    )
    return total[:, None]


def solution(mesh):
    paths = Paths(mesh.shape["row"], mesh.shape["col"])
    return jax.shard_map(
        functools.partial(local, paths),
        mesh=mesh,
        in_specs=(
            P("row", "col", None, None, None),
            P("row", "col", None),
            P("row", "col", None, None, None),
            P("row", "col", None),
            P("row", "col", None),
        ),
        out_specs=P("row", "col", None, None, None),
        check_vma=False,
    )
```
